512 devices in a mesh: gx: 8 (over z), gy: 8 (over x, core), gz: 8 (over y).
Axes of the slice: x: 4, y: 8, z: 8, core: 2. Of those that a mesh axis runs over, the one named last changes fastest.
Arguments:
- offsets: float32 [3, 64, 64, 64, 128], P(None, 'gx', 'gy', 'gz'), may hold values from 0 to 1
- velocity: float32 [3, 64, 64, 64, 128], P(None, 'gx', 'gy', 'gz'), may hold values from -6 to 6
- mass: float32 [64, 64, 64, 128], P('gx', 'gy', 'gz'), may hold values from 0.5 to 2
- support: float32 [64, 64, 64, 128], P('gx', 'gy', 'gz'), may hold values from 0.5 to 1
- energy: float32 [64, 64, 64, 128], P('gx', 'gy', 'gz'), may hold values from 0.5 to 2
- old_density: float32 [64, 64, 64, 128], P('gx', 'gy', 'gz'), may hold values from 0.5 to 2
- active_cells: int32 [8, 8, 8, 16], replicated, may hold values from 0 to 511, as said below
- active_count: int32 [8, 8, 8], replicated, may hold values from 1 to 16, as said below
Outputs:
- new_density: float32 [8, 8, 8, 16, 128], P('gx', 'gy', 'gz')
- acceleration: float32 [3, 8, 8, 8, 16, 128], P(None, 'gx', 'gy', 'gz')
- heating: float32 [8, 8, 8, 16, 128], P('gx', 'gy', 'gz')
The draws below stay inside these ranges and needn't reach their ends.
Inputs may be any that keep to these rules, and one draw needn't show every extreme that they name: `active_cells`: within each brick the 16 entries are distinct local cell numbers; only the first active_count entries of a brick are used. `active_count`: some brick uses all 16 slots.
All inputs are finite; a program needn't handle non-finite values.
Results may differ from the reference program's by a relative error of at most 0.00002.
Values sent between devices are 32-bit elements; how exact they have to be, the bound alone decides.
No kernel may reach another device: no remote copies, remote signals or barrier semaphores. Data moves between devices by JAX's collectives and lax.ppermute only.
A program may use at most 64 MiB of HBM per device.

```python
import math
import jax
import jax.numpy as jnp
from jax import lax

BX = 8
BY = 8
BZ = 8
ACT = 16
TILE = 128
NCX = 64
NCY = 64
NCZ = 64
N_GX = 8
N_GY = 8
N_GZ = 8


def draw_active_cells(key, part):
    key = jax.random.fold_in(key, 7)
    device_keys = jax.random.split(key, N_GX * N_GY * N_GZ)
    chosen = jax.vmap(lambda one_key: jax.random.permutation(one_key, BX * BY * BZ)[:ACT])(device_keys)
    return chosen.reshape(N_GX, N_GY, N_GZ, ACT).astype(jnp.int32)


def draw_active_count(key, part):
    key = jax.random.fold_in(key, 13)
    first_key, second_key = jax.random.split(key)
    halvings = jax.random.randint(first_key, (N_GX * N_GY * N_GZ,), 0, 4)
    counts = jnp.maximum(ACT // 2 ** halvings, 1)
    busiest = jax.random.randint(second_key, (), 0, N_GX * N_GY * N_GZ)
    counts = counts.at[busiest].set(ACT)
    return counts.reshape(N_GX, N_GY, N_GZ).astype(jnp.int32)


def block_scale(own_key, extent, shards, low, top_value):
    def one(position, parts):
        heights = jax.random.uniform(jax.random.fold_in(jax.random.fold_in(own_key, 6), position), (parts,), jnp.float32, low / len(shards), top_value / len(shards))
        return jnp.repeat(jnp.exp(heights), extent[position] // parts).reshape((-1,) + (1,) * (len(extent) - position - 1))

    factor_of = one(*shards[0])
    for cut in shards[1:]:
        factor_of = factor_of * one(*cut)
    return factor_of


def gaussian(rng, extent, deviation, most, cuts=(), held_as=jnp.bfloat16):
    drawn = deviation * jax.random.normal(rng, extent, jnp.float32)
    if cuts:
        drawn = drawn * block_scale(rng, extent, cuts, -0.22, 0.18)
    return jnp.clip(drawn, -most, most).astype(held_as)


def setup_inputs(seed: int = 0) -> dict:
    arg_keys = jax.random.split(jax.random.key(seed), 9)
    offsets = jnp.clip(1.0 * jax.random.uniform(arg_keys[0], (3, NCX, NCY, NCZ, TILE), jnp.float32) ** block_scale(arg_keys[0], (3, NCX, NCY, NCZ, TILE), ((1, 8), (2, 8), (3, 8)), -0.2, 0.2), 0.0, 1.0)
    velocity = gaussian(arg_keys[1], (3, NCX, NCY, NCZ, TILE), 1.0, 6.0, ((1, 8), (2, 8), (3, 8)), jnp.float32)
    mass = jnp.clip(jnp.exp(math.log(2.0) - 1.3862944 * jax.random.uniform(arg_keys[2], (NCX, NCY, NCZ, TILE), jnp.float32) ** block_scale(arg_keys[2], (NCX, NCY, NCZ, TILE), ((0, 8), (1, 8), (2, 8)), -0.2, 0.2)), 0.5, 2.0)
    support = jnp.clip(jnp.exp(math.log(1.0) - 0.6931472 * jax.random.uniform(arg_keys[3], (NCX, NCY, NCZ, TILE), jnp.float32) ** block_scale(arg_keys[3], (NCX, NCY, NCZ, TILE), ((0, 8), (1, 8), (2, 8)), -0.2, 0.2)), 0.5, 1.0)
    energy = jnp.clip(jnp.exp(math.log(2.0) - 1.3862944 * jax.random.uniform(arg_keys[4], (NCX, NCY, NCZ, TILE), jnp.float32) ** block_scale(arg_keys[4], (NCX, NCY, NCZ, TILE), ((0, 8), (1, 8), (2, 8)), -0.2, 0.2)), 0.5, 2.0)
    old_density = jnp.clip(jnp.exp(math.log(2.0) - 1.3862944 * jax.random.uniform(arg_keys[5], (NCX, NCY, NCZ, TILE), jnp.float32) ** block_scale(arg_keys[5], (NCX, NCY, NCZ, TILE), ((0, 8), (1, 8), (2, 8)), -0.2, 0.2)), 0.5, 2.0)
    active_cells = draw_active_cells(jax.random.fold_in(arg_keys[8], 71), 0)
    active_count = draw_active_count(jax.random.fold_in(arg_keys[8], 71), 0)
    return dict(offsets=offsets, velocity=velocity, mass=mass, support=support, energy=energy, old_density=old_density, active_cells=active_cells, active_count=active_count)


adiabatic_less_one = 2.0 / 3.0
kernel_norm = 21.0 / (2.0 * math.pi)

def neighbour_shifts():
    counter = jnp.arange(27, dtype=jnp.int32)
    return jnp.stack([counter // 9 - 1, counter // 3 % 3 - 1, counter % 3 - 1])

def separations(region):
    tile_size = region.shape[2]
    shifts = neighbour_shifts().astype(jnp.float32)
    centre = region[0:3, 13, :]
    others = (region[0:3] + shifts[:, :, None]).reshape(3, 27 * tile_size)
    return centre[:, None, :] - others[:, :, None]

def density_sum(region):
    tile_size = region.shape[2]
    separation = separations(region)
    distance = jnp.sqrt(lax.optimization_barrier(jnp.sum(separation * separation, axis=0)))
    radius = region[7, 13, :][None, :]
    scaled = distance / radius
    remain = jnp.maximum(1.0 - scaled, 0.0)
    kernel = kernel_norm / radius ** 3 * remain ** 4 * (1.0 + 4.0 * scaled)
    masses = region[6].reshape(-1)[:, None]
    return lax.optimization_barrier(jnp.sum(masses * kernel, axis=0)) / tile_size

def kernel_slope(distance, radius):
    remain = jnp.maximum(1.0 - distance / radius, 0.0)
    return -20.0 * kernel_norm / radius ** 5 * remain ** 3

def force_sums(region, current):
    tile_size = region.shape[2]
    separation = separations(region)
    distance = jnp.sqrt(lax.optimization_barrier(jnp.sum(separation * separation, axis=0)))
    pressure_term = adiabatic_less_one * region[8] / current
    own_term = pressure_term[13][None, :]
    other_term = pressure_term.reshape(-1)[:, None]
    own_slope = kernel_slope(distance, region[7, 13, :][None, :])
    other_slope = kernel_slope(distance, region[7].reshape(-1)[:, None])
    masses = region[6].reshape(-1)[:, None]
    factor = masses * (own_term * own_slope + other_term * other_slope)
    acceleration = -lax.optimization_barrier(jnp.sum(factor[None] * separation, axis=1)) / tile_size
    moving = region[3:6, 13, :][:, None, :] - region[3:6].reshape(3, -1)[:, :, None]
    closing = lax.optimization_barrier(jnp.sum(moving * separation, axis=0))
    heating = own_term[0] * lax.optimization_barrier(jnp.sum(masses * own_slope * closing, axis=0)) / tile_size
    return (acceleration, heating)

def region_at(source, location):
    zero_index = jnp.zeros((), jnp.int32)
    piece = lax.dynamic_slice(source, (zero_index, location[0], location[1], location[2], zero_index), (source.shape[0], 3, 3, 3, source.shape[4]))
    return piece.reshape(source.shape[0], 27, source.shape[4])

def reference(offsets, velocity, mass, support, energy, old_density, active_cells, active_count):
    fields = jnp.concatenate([offsets, velocity, mass[None], support[None], energy[None]], axis=0)
    widths = ((0, 0), (1, 1), (1, 1), (1, 1), (0, 0))
    padded = jnp.pad(fields, widths, mode='wrap')
    device_total = N_GX * N_GY * N_GZ
    flat_cells = active_cells.reshape(-1).astype(jnp.int32)
    slot_index = jnp.arange(device_total * ACT, dtype=jnp.int32)
    owner_index = slot_index // ACT
    usable = slot_index % ACT < active_count.reshape(-1)[owner_index]
    cell_x = owner_index // (N_GY * N_GZ) * BX + flat_cells // (BY * BZ)
    cell_y = owner_index // N_GZ % N_GY * BY + flat_cells // BZ % BY
    cell_z = owner_index % N_GZ * BZ + flat_cells % BZ
    locations = jnp.stack([cell_x, cell_y, cell_z], axis=1).astype(jnp.int32)
    renewed = lax.map(lambda location: density_sum(region_at(padded, location)), locations)
    renewed = jnp.where(usable[:, None], renewed, 0.0)
    cell_total = NCX * NCY * NCZ
    target = jnp.where(usable, (cell_x * NCY + cell_y) * NCZ + cell_z, cell_total).astype(jnp.int32)
    current = old_density.reshape(cell_total, TILE).at[target].set(renewed, mode='drop').reshape(old_density.shape)
    current_padded = jnp.pad(current[None], widths, mode='wrap')

    def force_at(location):
        return force_sums(region_at(padded, location), region_at(current_padded, location)[0])
    acceleration, heating = lax.map(force_at, locations)
    acceleration = jnp.where(usable[:, None, None], acceleration, 0.0)
    heating = jnp.where(usable[:, None], heating, 0.0)
    shape_out = (N_GX, N_GY, N_GZ, ACT, TILE)
    return (renewed.reshape(shape_out), jnp.moveaxis(acceleration, 1, 0).reshape((3,) + shape_out), heating.reshape(shape_out))
```

```python
import functools
import math

import jax
import jax.numpy as jnp
from jax import lax
from jax.experimental import pallas as pl
from jax.experimental.pallas import tpu as pltpu
from jax.sharding import PartitionSpec as P

BRICK = 8
WIDE = BRICK + 4
NEAR = BRICK + 2
ROW = 16
SLOTS = 16
TILE = 128
A_ROWS = WIDE * WIDE * WIDE * 4
B_ROWS = NEAR * NEAR * WIDE * 4
P_ROWS = NEAR * NEAR * ROW
X_ROWS = 2 * 64 * 4 + 64 * 4 + 64
Z_ROWS = 96 * 8 + 80 * 4 + 80
Y_ROWS = 12 * 96 + 10 * 48 + 10 * 16
PAIRS = 512
FAR = 16 * 1024 * 1024
LIMIT = 16 * 1024 * 1024

adiabatic_less_one = 2.0 / 3.0
kernel_norm = 21.0 / (2.0 * math.pi)
density_scale = kernel_norm / (256.0 * TILE)
slope_scale = 20.0 * kernel_norm / (64.0 * TILE)
TINY = 1e-30

bf16 = jnp.bfloat16
f32 = jnp.float32


def a_row(x, y, z):
    return ((x * WIDE + y) * WIDE + z) * 4


def b_row(x, y, z):
    return ((x * NEAR + y) * WIDE + z) * 4


def p_row(x, y, z):
    return (x * NEAR + y) * ROW + ((z + 7) & 15)


def near_id(x, y, z):
    return (x * NEAR + y) * NEAR + z


def rows(ref, start, size, multiple=4):
    return ref[pl.ds(pl.multiple_of(start, multiple), size), :]


def put(ref, start, value, multiple=4):
    ref[pl.ds(pl.multiple_of(start, multiple), value.shape[0]), :] = value


def move(to, to_row, source, row, size):
    to[to_row : to_row + size, :] = source[row : row + size, :]


def pack_x(
    where, cells, counts, fields, own, count, near_counts, near_cells, ta, tb, tp, up, down, held, count_tiles, own_tile, sems
):
    copies = [pltpu.make_async_copy(field, place, sems.at[k]) for k, (field, place) in enumerate(zip(fields, held))]
    for copy in copies:
        copy.start()
    lists = []
    for k in range(9):
        a, b = (where[0] + k // 3 - 1) & 7, (where[1] + k % 3 - 1) & 7
        lists.append(pltpu.make_async_copy(cells.at[a, b], near_cells.at[k], sems.at[6 + k]))
        if k % 3 == 0:
            lists.append(pltpu.make_async_copy(counts.at[a], count_tiles.at[k // 3], sems.at[15 + k // 3]))
    own_copy = pltpu.make_async_copy(cells.at[where[0], where[1]], own_tile, sems.at[18])
    lists.append(own_copy)
    for copy in lists:
        copy.start()
    for copy in lists:
        copy.wait()
    for s in range(SLOTS):
        own[s] = own_tile[where[2], s]
    for k in range(27):
        b, d = (where[1] + k // 3 % 3 - 1) & 7, (where[2] + k % 3 - 1) & 7
        near_counts[k] = count_tiles[k // 9, b, d]
    count[0] = near_counts[13]
    for copy in copies:
        copy.wait()
    off, vel, mass, sup, energy, old = held
    for x in range(BRICK):
        for y in range(BRICK):
            a, b = a_row(x + 2, y + 2, 2), b_row(x + 1, y + 1, 2)
            for f in range(3):
                ta[pl.ds(a + f, BRICK, stride=4), :] = off[f, x, y] - 0.5
                tb[pl.ds(b + f, BRICK, stride=4), :] = vel[f, x, y]
            ta[pl.ds(a + 3, BRICK, stride=4), :] = mass[x, y]
            tb[pl.ds(b + 3, BRICK, stride=4), :] = sup[x, y]
            p = p_row(x + 1, y + 1, 1)
            tp[p : p + BRICK, :] = adiabatic_less_one * energy[x, y] / old[x, y]

    def slot(s, carry):
        x, y, z = slot_place(own, s)
        tp[pl.ds(p_row(x + 1, y + 1, z + 1), 1), :] = -energy[x, y, pl.ds(z, 1), :]
        return carry

    lax.fori_loop(0, count[0], slot, 0)
    for ref, xa, xb in ((up, 8, 8), (down, 2, 1)):
        for y in range(BRICK):
            for layer in range(2):
                move(ref, (layer * 8 + y) * 32, ta, a_row(xa + layer, y + 2, 2), 32)
            move(ref, 512 + y * 32, tb, b_row(xb, y + 1, 2), 32)
            move(ref, 768 + y * 8, tp, p_row(xb, y + 1, 1), 8)


def fill_x(low, high, ta, tb, tp):
    for ref, xa, xb in ((low, 0, 0), (high, 10, 9)):
        for y in range(BRICK):
            for layer in range(2):
                move(ta, a_row(xa + layer, y + 2, 2), ref, (layer * 8 + y) * 32, 32)
            move(tb, b_row(xb, y + 1, 2), ref, 512 + y * 32, 32)
            move(tp, p_row(xb, y + 1, 1), ref, 768 + y * 8, 8)


def pack_z(ta, tb, tp, up, down):
    for ref, za, zb, zp in ((up, 8, 9, 8), (down, 2, 2, 1)):
        for i in range(96):
            move(ref, i * 8, ta, a_row(i // 8, i % 8 + 2, za), 8)
        for i in range(80):
            move(ref, 768 + i * 4, tb, b_row(i // 8, i % 8 + 1, zb), 4)
            move(ref, 1088 + i, tp, p_row(i // 8, i % 8 + 1, zp), 1)


def fill_z(low, high, ta, tb, tp):
    for ref, za, zb, zp in ((low, 0, 1, 0), (high, 10, 10, 9)):
        for i in range(96):
            move(ta, a_row(i // 8, i % 8 + 2, za), ref, i * 8, 8)
        for i in range(80):
            move(tb, b_row(i // 8, i % 8 + 1, zb), ref, 768 + i * 4, 4)
            move(tp, p_row(i // 8, i % 8 + 1, zp), ref, 1088 + i, 1)


def pack_y(ta, tb, tp, up, down):
    for ref, ya, yb in ((up, 8, 8), (down, 2, 1)):
        for x in range(WIDE):
            move(ref, x * 96, ta, a_row(x, ya, 0), 96)
        for x in range(NEAR):
            move(ref, 1152 + x * 48, tb, b_row(x, yb, 0), 48)
            move(ref, 1632 + x * 16, tp, (x * NEAR + yb) * ROW, 16)


def fill_y(low, high, ta, tb, tp):
    for ref, ya, yb in ((low, 0, 0), (high, 10, 9)):
        for x in range(WIDE):
            move(ta, a_row(x, ya, 0), ref, x * 96, 96)
        for x in range(NEAR):
            move(tb, b_row(x, yb, 0), ref, 1152 + x * 48, 48)
            move(tp, (x * NEAR + yb) * ROW, ref, 1632 + x * 16, 16)


def thirds(value):
    high = value.astype(bf16).astype(f32)
    rest = value - high
    middle = rest.astype(bf16).astype(f32)
    return high, middle, rest - middle


def own_side(position, support):
    x, y, z = position[0:1], position[1:2], position[2:3]
    square = x * x + y * y + z * z
    zero = jnp.zeros((3, TILE), f32)
    eight = jnp.concatenate(
        [-32.0 * x, -32.0 * y, -32.0 * z, jnp.full((1, TILE), 16.0, f32), 16.0 * square, zero], axis=0
    )
    first, second, third = thirds(eight)
    four = jnp.concatenate([4.0 * support, jnp.zeros((7, TILE), f32)], axis=0)
    filler = jnp.zeros((TILE - 56, TILE), f32)
    stacked = jnp.concatenate([first, first, first, second, second, third, four, filler], axis=0)
    turned = stacked.T
    reach = jnp.broadcast_to(turned[:, 48:49], (TILE, TILE))
    return turned[:, 0:48].astype(bf16), reach


def distances(square):
    square = jnp.maximum(square, TINY)
    return square * lax.rsqrt(square)


def halves(value):
    high = value.astype(bf16)
    return high, (value - high.astype(f32)).astype(bf16)


def contract(columns, weights):
    return lax.dot_general(columns, weights, (((1,), (1,)), ((), ())), preferred_element_type=f32)


def wide(parts):
    return jnp.concatenate(parts, axis=1)


def tall(parts):
    return jnp.concatenate(parts, axis=0)


def eighth_power(value):
    value = value * value
    value = value * value
    return value * value


def slot_place(own, s):
    cell = own[s]
    return cell >> 6, (cell >> 3) & 7, cell & 7


def lane_sums(value):
    return jnp.sum(value.T, axis=0, keepdims=True)


def place_rows(dx, dy, dz, rank):
    fx, fy, fz = (jnp.asarray(d).astype(f32) for d in (dx, dy, dz))
    return jnp.where(rank == 0, fx, jnp.where(rank == 1, fy, jnp.where(rank == 2, fz, 0.0)))


def other_side(position, eight, rank):
    square = jnp.sum(jnp.where(rank < 3, position * position, 0.0), axis=0, keepdims=True)
    line = lax.broadcasted_iota(jnp.int32, (8, TILE), 0)
    mixed = jnp.where(line < 3, eight, jnp.where(line == 3, square, jnp.where(line == 4, 1.0, 0.0)))
    first, second, third = thirds(mixed)
    return tall([first, second, third, first, second, first]).astype(bf16)


def weigh(weight, base):
    return tall(thirds(weight * base)).astype(bf16)


NEIGHBOURS = [(dx, dy, dz) for dx in (-1, 0, 1) for dy in (-1, 0, 1) for dz in (-1, 0, 1)]
PIECE = 32


def prepare_slots(own, ta, tb, lefts, reaches, supports):
    def group(g, carry):
        for k in range(4):
            s = g * 4 + k
            x, y, z = slot_place(own, s)
            position = rows(ta, a_row(x + 2, y + 2, z + 2), 4)
            support = rows(tb, b_row(x + 1, y + 1, z + 2), 4)[3:4]
            left, reach = own_side(position[0:3], support)
            lefts[s] = left
            reaches[s] = reach
            supports[s] = 0.25 * reach
        return carry

    lax.fori_loop(0, SLOTS // 4, group, 0)


def slot_sums(own, ta, tb, tp, lefts, reaches, supports, sums, s):
    x, y, z = slot_place(own, s)
    rank = lax.broadcasted_iota(jnp.int32, (4, TILE), 0)
    line = lax.broadcasted_iota(jnp.int32, (8, TILE), 0)
    centre = rows(tb, b_row(x + 1, y + 1, z + 2), 4)
    drift = jnp.where(rank < 3, jnp.mean(centre, axis=1, keepdims=True), 0.0)
    left = lefts[s]
    total = jnp.zeros((TILE, TILE), f32)
    a_columns, b_columns, a_weights, b_weights, sides = [], [], [], [], []
    for dx, dy, dz in NEIGHBOURS:
        position = rows(ta, a_row(x + 2 + dx, y + 2 + dy, z + 2 + dz), 4) + place_rows(dx, dy, dz, rank)
        motion = rows(tb, b_row(x + 1 + dx, y + 1 + dy, z + 2 + dz), 4) - drift
        mass, support = position[3:4], motion[3:4]
        pressure = tp[pl.ds(p_row(x + 1 + dx, y + 1 + dy, z + 1 + dz), 1), :]
        still = jnp.maximum(pressure, 0.0)
        inner = jnp.sum(jnp.where(rank < 3, position * motion, 0.0), axis=0, keepdims=True)
        eight = tall([position, motion])
        base = jnp.where(line == 3, 1.0, jnp.where(line == 7, inner, eight))
        a_columns += [weigh(mass, base)] * 2
        b_columns += [weigh(mass * still / eighth_power(support), base)] * 2
        sides.append((other_side(position, eight, rank), mass, 4.0 * support))
    for k, (side, mass, support) in enumerate(sides):
        if k % 2 == 0:
            pair = wide([side, sides[k + 1][0]]) if k + 1 < 27 else side
            both = jnp.dot(left, pair, preferred_element_type=f32)
        squares = both[:, (k % 2) * TILE : (k % 2 + 1) * TILE]
        terms, a_high, a_low, b_high, b_low = [], [], [], [], []
        for r in range(0, TILE, PIECE):
            reach = reaches[s, r : r + PIECE, :]
            distance = distances(squares[r : r + PIECE])
            inside = jnp.maximum(reach - distance, 0.0)
            square = inside * inside
            terms.append(square * square * (distance + supports[s, r : r + PIECE, :]) * mass)
            high, low = halves(square * inside)
            a_high.append(high)
            a_low.append(low)
            outer = jnp.maximum(support - distance, 0.0)
            high, low = halves(outer * outer * outer)
            b_high.append(high)
            b_low.append(low)
        total = total + tall(terms)
        a_weights += [tall(a_high), tall(a_low)]
        b_weights += [tall(b_high), tall(b_low)]
    a_sum = contract(wide(a_columns), wide(a_weights))
    b_sum = contract(wide(b_columns), wide(b_weights))
    at = s * 16
    put(sums, at, a_sum[0:8] + a_sum[8:16] + a_sum[16:24], 8)
    put(sums, at + 8, b_sum[0:8] + b_sum[8:16] + b_sum[16:24], 8)
    sums[pl.ds(at + 15, 1), :] = density_scale * lane_sums(total) / eighth_power(centre[3:4])


def active_pairs(pairs, own, ta, tb, tp, lefts, sums, first, size):
    rank = lax.broadcasted_iota(jnp.int32, (4, TILE), 0)
    line = lax.broadcasted_iota(jnp.int32, (8, TILE), 0)
    found = []
    for k in range(size):
        pair = pairs[first + k]
        s, n = pair >> 5, pair & 31
        x, y, z = slot_place(own, s & 15)
        dx, dy, dz = n // 9 - 1, n // 3 % 3 - 1, n % 3 - 1
        position = rows(ta, a_row(x + 2 + dx, y + 2 + dy, z + 2 + dz), 4) + place_rows(dx, dy, dz, rank)
        support = rows(tb, b_row(x + 1 + dx, y + 1 + dy, z + 2 + dz), 4)[3:4]
        pressure = tp[pl.ds(p_row(x + 1 + dx, y + 1 + dy, z + 1 + dz), 1), :]
        eight = tall([position, jnp.zeros((4, TILE), f32)])
        base = jnp.where(line < 3, eight, jnp.where(line == 6, 1.0, 0.0))
        base = jnp.where(line == 3, 1.0, jnp.where(line < 3, base, 0.0))
        columns = weigh(position[3:4] * pressure / eighth_power(support), base)
        squares = jnp.dot(lefts[s & 15], other_side(position, eight, rank), preferred_element_type=f32)
        outer = jnp.maximum(4.0 * support - distances(squares), 0.0)
        high, low = halves(outer * outer * outer)
        out = contract(wide([columns, columns]), wide([high, low]))
        found.append((s, out[0:8] + out[8:16] + out[16:24]))
    for s, more in found:
        sums[pl.ds(pl.multiple_of(s * 16 + 8, 8), 4), :] += more[0:4]


def halo_density(ta, tb, tp, x, y, z):
    rank = lax.broadcasted_iota(jnp.int32, (4, TILE), 0)
    centre = rows(ta, a_row(x + 1, y + 1, z + 1), 4)
    support = rows(tb, b_row(x, y, z + 1), 4)[3:4]
    left, reach = own_side(centre[0:3], support)
    total = jnp.zeros((TILE, TILE), f32)
    sides = []
    for dx, dy, dz in NEIGHBOURS:
        position = rows(ta, a_row(x + 1 + dx, y + 1 + dy, z + 1 + dz), 4) + place_rows(dx, dy, dz, rank)
        eight = tall([position, jnp.zeros((4, TILE), f32)])
        sides.append((other_side(position, eight, rank), position[3:4]))
    for k, (side, mass) in enumerate(sides):
        if k % 2 == 0:
            pair = wide([side, sides[k + 1][0]]) if k + 1 < 27 else side
            both = jnp.dot(left, pair, preferred_element_type=f32)
        squares = both[:, (k % 2) * TILE : (k % 2 + 1) * TILE]
        terms = []
        for r in range(0, TILE, PIECE):
            near = reach[r : r + PIECE]
            distance = distances(squares[r : r + PIECE])
            inside = jnp.maximum(near - distance, 0.0)
            square = inside * inside
            terms.append(square * square * (distance + 0.25 * near) * mass)
        total = total + tall(terms)
    density = density_scale * lane_sums(total) / eighth_power(support)
    at = p_row(x, y, z)
    tp[pl.ds(at, 1), :] = -adiabatic_less_one * tp[pl.ds(at, 1), :] / density


def mark_near(where, own, own_count, near_cells, near_counts, marks):
    brick_z = lax.broadcasted_iota(jnp.int32, (BRICK, SLOTS), 0)
    place = lax.broadcasted_iota(jnp.int32, (BRICK, SLOTS), 1)
    dz = ((brick_z - where[2] + 9) & 7) - 1
    listed = []
    for k in range(9):
        cell = near_cells[k]
        counts = [jnp.where(dz == d, near_counts[k * 3 + d + 1], 0) for d in (-1, 0, 1)]
        used = place < counts[0] + counts[1] + counts[2]
        x = (cell >> 6) + (k // 3 - 1) * BRICK
        y = ((cell >> 3) & 7) + (k % 3 - 1) * BRICK
        listed.append((jnp.where(used, x, -99), y, (cell & 7) + dz * BRICK, cell))

    def slot(s, bits):
        ox, oy, oz = slot_place(own, s)
        out = []
        for (x, y, z, _), bit in zip(listed, bits):
            far = jnp.maximum(jnp.maximum(jnp.abs(x - ox), jnp.abs(y - oy)), jnp.abs(z - oz))
            out.append(bit | jnp.where(far <= 1, jnp.left_shift(1, s), 0))
        return tuple(out)

    bits = lax.fori_loop(0, own_count, slot, (jnp.zeros((BRICK, SLOTS), jnp.int32),) * 9)
    for k in range(9):
        marks[k] = jnp.where(bits[k] == 0, 0, bits[k] | (listed[k][3] << 16))


def list_near(where, own, own_count, marks, found, found_count, pairs, pair_count):
    found_count[0] = 0
    pair_count[0] = 0

    def brick(b, carry):
        k = b // 3
        dx, dy, dz = k // 3 - 1, k % 3 - 1, b % 3 - 1
        level = (where[2] + dz) & 7

        def take(mark):
            cell = mark >> 16
            x, y, z = (cell >> 6) + dx * BRICK, ((cell >> 3) & 7) + dy * BRICK, (cell & 7) + dz * BRICK

            @pl.when(b != 13)
            def _():
                at = found_count[0]
                found[at] = near_id(x + 1, y + 1, z + 1)
                found_count[0] = at + 1

            def slot(s, carry):
                @pl.when(((mark >> s) & 1) == 1)
                def _():
                    ox, oy, oz = slot_place(own, s)
                    at = pair_count[0]
                    pairs[at] = s * 32 + (x - ox + 1) * 9 + (y - oy + 1) * 3 + z - oz + 1
                    pair_count[0] = at + 1

                return carry

            lax.fori_loop(0, own_count, slot, 0)

        for first in range(0, SLOTS, 4):
            four = [marks[k, level, first + i] for i in range(4)]

            @pl.when((four[0] | four[1] | four[2] | four[3]) != 0)
            def _():
                for mark in four:
                    pl.when(mark != 0)(functools.partial(take, mark))

        return carry

    lax.fori_loop(0, 27, brick, 0)
    for k in range(4):
        pairs[pair_count[0] + k] = SLOTS * 32 + 13


def run_stage(stage, quota, own, count, ta, tb, tp, lefts, reaches, supports, done, sums):
    edge = lambda v: (v == 0) | (v == BRICK - 1)

    def slot(s, taken):
        x, y, z = slot_place(own, s)
        need = jnp.where(edge(y), 3, jnp.where(edge(z), 2, jnp.where(edge(x), 1, 0)))
        go = (need <= stage) & (done[s] == 0) & (taken < quota)

        @pl.when(go)
        def _():
            slot_sums(own, ta, tb, tp, lefts, reaches, supports, sums, s)
            done[s] = 1

        return taken + go.astype(jnp.int32)

    lax.fori_loop(0, count[0], slot, jnp.int32(0))


def finish_slot(own, count, ta, tb, tp, sums, s, density_out, acceleration_out, heating_out):
    used = s < count[0]
    keep = lambda value: jnp.where(used, value, 0.0)
    x, y, z = slot_place(own, s)
    centre_a = rows(ta, a_row(x + 2, y + 2, z + 2), 4)
    centre_b = rows(tb, b_row(x + 1, y + 1, z + 2), 4)
    a_sum = rows(sums, s * 16, 8, 8)
    b_sum = rows(sums, s * 16 + 8, 8, 8)
    pressure = tp[pl.ds(p_row(x + 1, y + 1, z + 1), 1), :]
    own_scale = slope_scale * pressure / eighth_power(centre_b[3:4])
    moving = centre_b - jnp.mean(centre_b, axis=1, keepdims=True)
    heat = a_sum[7:8]
    inner = jnp.zeros((1, TILE), f32)
    for f in range(3):
        position, speed = centre_a[f : f + 1], moving[f : f + 1]
        inner = inner + position * speed
        heat = heat - speed * a_sum[f : f + 1] - position * a_sum[4 + f : 5 + f]
        push = own_scale * (position * a_sum[3:4] - a_sum[f : f + 1])
        push = push + slope_scale * (position * b_sum[3:4] - b_sum[f : f + 1])
        acceleration_out[f, pl.ds(s, 1), :] = keep(push)
    heating_out[pl.ds(s, 1), :] = keep(-own_scale * (heat + inner * a_sum[3:4]))
    density_out[pl.ds(s, 1), :] = keep(b_sum[7:8])


SMEM = pltpu.SMEM
VMEM = pltpu.VMEM
i32 = jnp.int32


def call(body, name, inputs, outputs, aliases=(), scratch=(), flops=0, limit=LIMIT):
    return pl.pallas_call(
        body,
        name=name,
        out_shape=[jax.ShapeDtypeStruct(shape, dtype) for shape, dtype, _ in outputs],
        in_specs=[pl.BlockSpec(memory_space=space) for _, space in inputs],
        out_specs=[pl.BlockSpec(memory_space=space) for _, _, space in outputs],
        scratch_shapes=list(scratch),
        input_output_aliases=dict(aliases),
        compiler_params=pltpu.CompilerParams(vmem_limit_bytes=limit),
        cost_estimate=pl.CostEstimate(flops=flops, bytes_accessed=1 << 20, transcendentals=0),
    )(*[array for array, _ in inputs])


def pack_x_kernel(where, cells, counts, *refs):
    pack_x(where, cells, counts, refs[:6], *refs[6:15], refs[15:21], *refs[21:])


def stage0_kernel(
    own, count, near_counts, where, near_cells, ta_in, tb_in, tp_in,
    ta, tb, tp, marks, done, lefts, reaches, supports, sums,
):
    mark_near(where, own, count[0], near_cells, near_counts, marks)
    for s in range(SLOTS):
        done[s] = 0
    prepare_slots(own, ta, tb, lefts, reaches, supports)
    run_stage(0, QUOTAS[0], own, count, ta, tb, tp, lefts, reaches, supports, done, sums)


def stage1_kernel(
    own, count, where, marks, done_in, lefts, reaches, supports, ta_in, tb_in, tp_in, sums_in,
    ta, tb, tp, done, sums, found, found_count, pairs, pair_count,
):
    list_near(where, own, count[0], marks, found, found_count, pairs, pair_count)
    for s in range(SLOTS):
        done[s] = done_in[s]
    run_stage(1, QUOTAS[1], own, count, ta, tb, tp, lefts, reaches, supports, done, sums)


def stage2_kernel(
    own, count, done_in, lefts, reaches, supports, ta_in, tb_in, tp_in, sums_in, ta, tb, tp, done, sums
):
    for s in range(SLOTS):
        done[s] = done_in[s]
    run_stage(2, QUOTAS[2], own, count, ta, tb, tp, lefts, reaches, supports, done, sums)


def pack_kernel(fill, pack, low, high, ta_in, tb_in, tp_in, ta, tb, tp, up, down):
    fill(low, high, ta, tb, tp)
    pack(ta, tb, tp, up, down)


def last_kernel(
    own, count, done_in, found, found_count, pairs, pair_count, lefts, reaches, supports, yl, yh,
    ta_in, tb_in, tp_in, sums_in, density_out, acceleration_out, heating_out, ta, tb, tp, sums, done,
):
    fill_y(yl, yh, ta, tb, tp)
    for s in range(SLOTS):
        done[s] = done_in[s]
    run_stage(3, SLOTS, own, count, ta, tb, tp, lefts, reaches, supports, done, sums)

    def halo(k, carry):
        cell = found[k]
        halo_density(ta, tb, tp, cell // 100, cell // 10 % 10, cell % 10)
        return carry

    lax.fori_loop(0, found_count[0], halo, 0)

    def renew(g, carry):
        for s in (g * 4, g * 4 + 1, g * 4 + 2, g * 4 + 3):
            x, y, z = slot_place(own, s)
            at = p_row(x + 1, y + 1, z + 1)
            tp[pl.ds(at, 1), :] = -adiabatic_less_one * tp[pl.ds(at, 1), :] / sums[pl.ds(s * 16 + 15, 1), :]
        return carry

    lax.fori_loop(0, SLOTS // 4, renew, 0)

    def some_pairs(g, carry):
        active_pairs(pairs, own, ta, tb, tp, lefts, sums, g * 4, 4)
        return carry

    lax.fori_loop(0, (pair_count[0] + 3) // 4, some_pairs, 0)

    def finish(g, carry):
        for s in (g * 4, g * 4 + 1, g * 4 + 2, g * 4 + 3):
            finish_slot(own, count, ta, tb, tp, sums, s, density_out, acceleration_out, heating_out)
        return carry

    lax.fori_loop(0, SLOTS // 4, finish, 0)


QUOTAS = (4, 6, 5)


def shift_both(axis, up, down):
    devices = lax.axis_size(axis)
    higher = [(i, (i + 1) % devices) for i in range(devices)]
    lower = [(j, i) for i, j in higher]
    return lax.ppermute(up, axis, higher), lax.ppermute(down, axis, lower)


def on_device(offsets, velocity, mass, support, energy, old_density, active_cells, active_count):
    where = jnp.stack([lax.axis_index(a) for a in ("gx", "gy", "gz")]).astype(i32)
    grow = lambda n: ((n, TILE), f32, VMEM)
    tables = [grow(A_ROWS), grow(B_ROWS), grow(P_ROWS)]
    fields = [offsets, velocity, mass, support, energy, old_density]
    scalars = lambda n: ((n,), i32, SMEM)
    near_shape = ((9, BRICK, SLOTS), i32, VMEM)
    own, count, near_counts, near_cells, ta, tb, tp, up, down = call(
        pack_x_kernel, "pack_x",
        [(where, SMEM), (active_cells, pltpu.HBM), (active_count, pltpu.HBM)] + [(f, pltpu.HBM) for f in fields],
        [scalars(SLOTS), scalars(1), scalars(27), near_shape, *tables, grow(X_ROWS), grow(X_ROWS)],
        scratch=[VMEM(f.shape, f32) for f in fields]
        + [SMEM((3, BRICK, BRICK), i32), SMEM((BRICK, SLOTS), i32), pltpu.SemaphoreType.DMA((19,))],
        limit=FAR,
    )
    xl, xh = shift_both("gx", up, down)
    slot_tables = [((SLOTS, TILE, 48), bf16, VMEM), ((SLOTS, TILE, TILE), f32, VMEM), ((SLOTS, TILE, TILE), f32, VMEM)]
    sums_shape = grow((SLOTS + 1) * 16)
    ta, tb, tp, marks, done, lefts, reaches, supports, sums = call(
        stage0_kernel, "stage0",
        [(own, SMEM), (count, SMEM), (near_counts, SMEM), (where, SMEM)]
        + [(near_cells, VMEM), (ta, VMEM), (tb, VMEM), (tp, VMEM)],
        [*tables, near_shape, scalars(SLOTS), *slot_tables, sums_shape],
        {5: 0, 6: 1, 7: 2}, flops=8_000_000_000,
    )

    def packed(fill, pack, name, low, high, ta, tb, tp, length):
        return call(
            functools.partial(pack_kernel, fill, pack), name, [(v, VMEM) for v in (low, high, ta, tb, tp)],
            [*tables, grow(length), grow(length)], {2: 0, 3: 1, 4: 2},
        )

    ta, tb, tp, up, down = packed(fill_x, pack_z, "pack_z", xl, xh, ta, tb, tp, Z_ROWS)
    zl, zh = shift_both("gz", up, down)
    ta, tb, tp, done, sums, *lists = call(
        stage1_kernel, "stage1",
        [(v, SMEM) for v in (own, count, where, marks, done)]
        + [(v, VMEM) for v in (lefts, reaches, supports, ta, tb, tp, sums)],
        [*tables, scalars(SLOTS), sums_shape, scalars(512), scalars(1), scalars(PAIRS), scalars(1)],
        {8: 0, 9: 1, 10: 2, 11: 4}, flops=8_000_000_000,
    )
    ta, tb, tp, up, down = packed(fill_z, pack_y, "pack_y", zl, zh, ta, tb, tp, Y_ROWS)
    yl, yh = shift_both("gy", up, down)
    ta, tb, tp, done, sums = call(
        stage2_kernel, "stage2",
        [(v, SMEM) for v in (own, count, done)] + [(v, VMEM) for v in (lefts, reaches, supports, ta, tb, tp, sums)],
        [*tables, scalars(SLOTS), sums_shape], {6: 0, 7: 1, 8: 2, 9: 4}, flops=8_000_000_000,
    )
    density, acceleration, heating, *_ = call(
        last_kernel, "last",
        [(v, SMEM) for v in (own, count, done, *lists)]
        + [(v, VMEM) for v in (lefts, reaches, supports, yl, yh, ta, tb, tp, sums)],
        [((SLOTS, TILE), f32, VMEM), ((3, SLOTS, TILE), f32, VMEM), ((SLOTS, TILE), f32, VMEM), *tables, sums_shape],
        {12: 3, 13: 4, 14: 5, 15: 6}, scratch=[SMEM((SLOTS,), i32)], flops=1_000_000_000,
    )
    shape_out = (1, 1, 1, SLOTS, TILE)
    return density.reshape(shape_out), acceleration.reshape((3,) + shape_out), heating.reshape(shape_out)


def solution(mesh):
    in_specs = (
        P(None, "gx", "gy", "gz", None),
        P(None, "gx", "gy", "gz", None),
        P("gx", "gy", "gz", None),
        P("gx", "gy", "gz", None),
        P("gx", "gy", "gz", None),
        P("gx", "gy", "gz", None),
        P(),
        P(),
    )
    out_specs = (
        P("gx", "gy", "gz", None, None),
        P(None, "gx", "gy", "gz", None, None),
        P("gx", "gy", "gz", None, None),
    )
    return jax.shard_map(
        on_device, mesh=mesh, in_specs=in_specs, out_specs=out_specs, check_vma=False
    )
```

```python
import functools
import math

import jax
import jax.numpy as jnp
from jax import lax
from jax.experimental import pallas as pl
from jax.experimental.pallas import tpu as pltpu
from jax.sharding import PartitionSpec as P

BRICK = 8
WIDE = BRICK + 4
NEAR = BRICK + 2
ROW = 16
SLOTS = 16
TILE = 128
A_ROWS = WIDE * WIDE * WIDE * 4
B_ROWS = NEAR * NEAR * WIDE * 4
P_ROWS = NEAR * NEAR * ROW
X_ROWS = 2 * 64 * 4 + 64 * 4 + 64
Z_ROWS = 96 * 8 + 80 * 4 + 80
Y_ROWS = 12 * 96 + 10 * 48 + 10 * 16
PAIRS = 512
GROUP = 8
LIMIT = 16 * 1024 * 1024

adiabatic_less_one = 2.0 / 3.0
kernel_norm = 21.0 / (2.0 * math.pi)
density_scale = kernel_norm / (256.0 * TILE)
slope_scale = 20.0 * kernel_norm / (64.0 * TILE)
TINY = 1e-30

bf16 = jnp.bfloat16
f32 = jnp.float32


def a_row(x, y, z):
    return ((x * WIDE + y) * WIDE + z) * 4


def b_row(x, y, z):
    return ((x * NEAR + y) * WIDE + z) * 4


def p_row(x, y, z):
    return (x * NEAR + y) * ROW + ((z + 7) & 15)


def near_id(x, y, z):
    return (x * NEAR + y) * NEAR + z


def rows(ref, start, size, multiple=4):
    return ref[pl.ds(pl.multiple_of(start, multiple), size), :]


def put(ref, start, value, multiple=4):
    ref[pl.ds(pl.multiple_of(start, multiple), value.shape[0]), :] = value


def move(to, to_row, source, row, size):
    to[to_row : to_row + size, :] = source[row : row + size, :]


def pack_x(
    where, cells, counts, fields, own, count, near_counts, near_cells, ta, tb, tp, up, down, held, count_tiles, own_tile, sems
):
    copies = [pltpu.make_async_copy(field, place, sems.at[k]) for k, (field, place) in enumerate(zip(fields, held))]
    for copy in copies:
        copy.start()
    lists = []
    for k in range(9):
        a, b = (where[0] + k // 3 - 1) & 7, (where[1] + k % 3 - 1) & 7
        lists.append(pltpu.make_async_copy(cells.at[a, b], near_cells.at[k], sems.at[6 + k]))
        if k % 3 == 0:
            lists.append(pltpu.make_async_copy(counts.at[a], count_tiles.at[k // 3], sems.at[15 + k // 3]))
    own_copy = pltpu.make_async_copy(cells.at[where[0], where[1]], own_tile, sems.at[18])
    lists.append(own_copy)
    for copy in lists:
        copy.start()
    for copy in lists:
        copy.wait()
    for s in range(SLOTS):
        own[s] = own_tile[where[2], s]
    for k in range(27):
        b, d = (where[1] + k // 3 % 3 - 1) & 7, (where[2] + k % 3 - 1) & 7
        near_counts[k] = count_tiles[k // 9, b, d]
    count[0] = near_counts[13]
    for copy in copies:
        copy.wait()
    off, vel, mass, sup, energy, old = held
    for x in range(BRICK):
        for y in range(BRICK):
            a, b = a_row(x + 2, y + 2, 2), b_row(x + 1, y + 1, 2)
            for f in range(3):
                ta[pl.ds(a + f, BRICK, stride=4), :] = off[f, x, y] - 0.5
                tb[pl.ds(b + f, BRICK, stride=4), :] = vel[f, x, y]
            ta[pl.ds(a + 3, BRICK, stride=4), :] = mass[x, y]
            tb[pl.ds(b + 3, BRICK, stride=4), :] = sup[x, y]
            p = p_row(x + 1, y + 1, 1)
            tp[p : p + BRICK, :] = adiabatic_less_one * energy[x, y] / old[x, y]

    def slot(s, carry):
        x, y, z = slot_place(own, s)
        tp[pl.ds(p_row(x + 1, y + 1, z + 1), 1), :] = -energy[x, y, pl.ds(z, 1), :]
        return carry

    lax.fori_loop(0, count[0], slot, 0)
    for ref, xa, xb in ((up, 8, 8), (down, 2, 1)):
        for y in range(BRICK):
            for layer in range(2):
                move(ref, (layer * 8 + y) * 32, ta, a_row(xa + layer, y + 2, 2), 32)
            move(ref, 512 + y * 32, tb, b_row(xb, y + 1, 2), 32)
            move(ref, 768 + y * 8, tp, p_row(xb, y + 1, 1), 8)


def fill_x(low, high, ta, tb, tp):
    for ref, xa, xb in ((low, 0, 0), (high, 10, 9)):
        for y in range(BRICK):
            for layer in range(2):
                move(ta, a_row(xa + layer, y + 2, 2), ref, (layer * 8 + y) * 32, 32)
            move(tb, b_row(xb, y + 1, 2), ref, 512 + y * 32, 32)
            move(tp, p_row(xb, y + 1, 1), ref, 768 + y * 8, 8)


def pack_z(ta, tb, tp, up, down):
    for ref, za, zb, zp in ((up, 8, 9, 8), (down, 2, 2, 1)):
        for i in range(96):
            move(ref, i * 8, ta, a_row(i // 8, i % 8 + 2, za), 8)
        for i in range(80):
            move(ref, 768 + i * 4, tb, b_row(i // 8, i % 8 + 1, zb), 4)
            move(ref, 1088 + i, tp, p_row(i // 8, i % 8 + 1, zp), 1)


def fill_z(low, high, ta, tb, tp):
    for ref, za, zb, zp in ((low, 0, 1, 0), (high, 10, 10, 9)):
        for i in range(96):
            move(ta, a_row(i // 8, i % 8 + 2, za), ref, i * 8, 8)
        for i in range(80):
            move(tb, b_row(i // 8, i % 8 + 1, zb), ref, 768 + i * 4, 4)
            move(tp, p_row(i // 8, i % 8 + 1, zp), ref, 1088 + i, 1)


def pack_y(ta, tb, tp, up, down):
    for ref, ya, yb in ((up, 8, 8), (down, 2, 1)):
        for x in range(WIDE):
            move(ref, x * 96, ta, a_row(x, ya, 0), 96)
        for x in range(NEAR):
            move(ref, 1152 + x * 48, tb, b_row(x, yb, 0), 48)
            move(ref, 1632 + x * 16, tp, (x * NEAR + yb) * ROW, 16)


def fill_y(low, high, ta, tb, tp):
    for ref, ya, yb in ((low, 0, 0), (high, 10, 9)):
        for x in range(WIDE):
            move(ta, a_row(x, ya, 0), ref, x * 96, 96)
        for x in range(NEAR):
            move(tb, b_row(x, yb, 0), ref, 1152 + x * 48, 48)
            move(tp, (x * NEAR + yb) * ROW, ref, 1632 + x * 16, 16)


def thirds(value):
    high = value.astype(bf16).astype(f32)
    rest = value - high
    middle = rest.astype(bf16).astype(f32)
    return high, middle, rest - middle


def own_side(position, support):
    x, y, z = position[0:1], position[1:2], position[2:3]
    square = x * x + y * y + z * z
    zero = jnp.zeros((3, TILE), f32)
    eight = jnp.concatenate(
        [-32.0 * x, -32.0 * y, -32.0 * z, jnp.full((1, TILE), 16.0, f32), 16.0 * square, zero], axis=0
    )
    first, second, third = thirds(eight)
    four = jnp.concatenate([4.0 * support, jnp.zeros((7, TILE), f32)], axis=0)
    filler = jnp.zeros((TILE - 56, TILE), f32)
    stacked = jnp.concatenate([first, first, first, second, second, third, four, filler], axis=0)
    turned = stacked.T
    reach = jnp.broadcast_to(turned[:, 48:49], (TILE, TILE))
    return turned[:, 0:48].astype(bf16), reach


def distances(square):
    square = jnp.maximum(square, TINY)
    return square * lax.rsqrt(square)


def halves(value):
    high = value.astype(bf16)
    return high, (value - high.astype(f32)).astype(bf16)


def contract(columns, weights):
    return lax.dot_general(columns, weights, (((1,), (1,)), ((), ())), preferred_element_type=f32)


def wide(parts):
    return jnp.concatenate(parts, axis=1)


def tall(parts):
    return jnp.concatenate(parts, axis=0)


def eighth_power(value):
    value = value * value
    value = value * value
    return value * value


def slot_place(own, s):
    cell = own[s]
    return cell >> 6, (cell >> 3) & 7, cell & 7


def lane_sums(value):
    return jnp.sum(value.T, axis=0, keepdims=True)


def place_rows(dx, dy, dz, rank):
    fx, fy, fz = (jnp.asarray(d).astype(f32) for d in (dx, dy, dz))
    return jnp.where(rank == 0, fx, jnp.where(rank == 1, fy, jnp.where(rank == 2, fz, 0.0)))


def other_side(position, eight, rank):
    square = jnp.sum(jnp.where(rank < 3, position * position, 0.0), axis=0, keepdims=True)
    line = lax.broadcasted_iota(jnp.int32, (8, TILE), 0)
    mixed = jnp.where(line < 3, eight, jnp.where(line == 3, square, jnp.where(line == 4, 1.0, 0.0)))
    first, second, third = thirds(mixed)
    return tall([first, second, third, first, second, first]).astype(bf16)


def weigh(weight, base):
    return tall(thirds(weight * base)).astype(bf16)


NEIGHBOURS = [(dx, dy, dz) for dx in (-1, 0, 1) for dy in (-1, 0, 1) for dz in (-1, 0, 1)]
PIECE = 32


def prepare_slots(own, ta, tb, lefts, reaches, supports):
    def group(g, carry):
        for k in range(4):
            s = g * 4 + k
            x, y, z = slot_place(own, s)
            position = rows(ta, a_row(x + 2, y + 2, z + 2), 4)
            support = rows(tb, b_row(x + 1, y + 1, z + 2), 4)[3:4]
            left, reach = own_side(position[0:3], support)
            lefts[s] = left
            reaches[s] = reach
            supports[s] = 0.25 * reach
        return carry

    lax.fori_loop(0, SLOTS // 4, group, 0)


def slot_sums(own, ta, tb, tp, lefts, reaches, supports, sums, s, planes, more):
    x, y, z = slot_place(own, s)
    rank = lax.broadcasted_iota(jnp.int32, (4, TILE), 0)
    line = lax.broadcasted_iota(jnp.int32, (8, TILE), 0)
    centre = rows(tb, b_row(x + 1, y + 1, z + 2), 4)
    drift = jnp.where(rank < 3, jnp.mean(centre, axis=1, keepdims=True), 0.0)
    left = lefts[s]
    total = jnp.zeros((TILE, TILE), f32)
    a_columns, b_columns, a_weights, b_weights, sides = [], [], [], [], []
    for dx, dy, dz in [(dx, dy, dz) for dy in planes for dx in (-1, 0, 1) for dz in (-1, 0, 1)]:
        position = rows(ta, a_row(x + 2 + dx, y + 2 + dy, z + 2 + dz), 4) + place_rows(dx, dy, dz, rank)
        motion = rows(tb, b_row(x + 1 + dx, y + 1 + dy, z + 2 + dz), 4) - drift
        mass, support = position[3:4], motion[3:4]
        pressure = tp[pl.ds(p_row(x + 1 + dx, y + 1 + dy, z + 1 + dz), 1), :]
        still = jnp.maximum(pressure, 0.0)
        inner = jnp.sum(jnp.where(rank < 3, position * motion, 0.0), axis=0, keepdims=True)
        eight = tall([position, motion])
        base = jnp.where(line == 3, 1.0, jnp.where(line == 7, inner, eight))
        a_columns += [weigh(mass, base)] * 2
        b_columns += [weigh(mass * still / eighth_power(support), base)] * 2
        sides.append((other_side(position, eight, rank), mass, 4.0 * support))
    for k, (side, mass, support) in enumerate(sides):
        if k % 2 == 0:
            pair = wide([side, sides[k + 1][0]]) if k + 1 < len(sides) else side
            both = jnp.dot(left, pair, preferred_element_type=f32)
        squares = both[:, (k % 2) * TILE : (k % 2 + 1) * TILE]
        terms, a_high, a_low, b_high, b_low = [], [], [], [], []
        for r in range(0, TILE, PIECE):
            reach = reaches[s, r : r + PIECE, :]
            distance = distances(squares[r : r + PIECE])
            inside = jnp.maximum(reach - distance, 0.0)
            square = inside * inside
            terms.append(square * square * (distance + supports[s, r : r + PIECE, :]) * mass)
            high, low = halves(square * inside)
            a_high.append(high)
            a_low.append(low)
            outer = jnp.maximum(support - distance, 0.0)
            high, low = halves(outer * outer * outer)
            b_high.append(high)
            b_low.append(low)
        total = total + tall(terms)
        a_weights += [tall(a_high), tall(a_low)]
        b_weights += [tall(b_high), tall(b_low)]
    a_sum = contract(wide(a_columns), wide(a_weights))
    b_sum = contract(wide(b_columns), wide(b_weights))
    at = s * 16
    a_sum = a_sum[0:8] + a_sum[8:16] + a_sum[16:24]
    b_sum = jnp.where(line == 7, lane_sums(total), b_sum[0:8] + b_sum[8:16] + b_sum[16:24])
    if more:
        a_sum = a_sum + rows(sums, at, 8, 8)
        b_sum = b_sum + rows(sums, at + 8, 8, 8)
    put(sums, at, a_sum, 8)
    put(sums, at + 8, b_sum, 8)


def active_pairs(pairs, own, ta, tb, tp, lefts, sums, first, size):
    rank = lax.broadcasted_iota(jnp.int32, (4, TILE), 0)
    line = lax.broadcasted_iota(jnp.int32, (8, TILE), 0)
    found = []
    for k in range(size):
        pair = pairs[first + k]
        s, n = pair >> 5, pair & 31
        x, y, z = slot_place(own, s & 15)
        dx, dy, dz = n // 9 - 1, n // 3 % 3 - 1, n % 3 - 1
        position = rows(ta, a_row(x + 2 + dx, y + 2 + dy, z + 2 + dz), 4) + place_rows(dx, dy, dz, rank)
        support = rows(tb, b_row(x + 1 + dx, y + 1 + dy, z + 2 + dz), 4)[3:4]
        pressure = jnp.abs(tp[pl.ds(p_row(x + 1 + dx, y + 1 + dy, z + 1 + dz), 1), :])
        eight = tall([position, jnp.zeros((4, TILE), f32)])
        base = jnp.where(line == 3, 1.0, jnp.where(line < 3, eight, 0.0))
        columns = weigh(position[3:4] * pressure / eighth_power(support), base)
        squares = jnp.dot(lefts[s & 15], other_side(position, eight, rank), preferred_element_type=f32)
        outer = jnp.maximum(4.0 * support - distances(squares), 0.0)
        high, low = halves(outer * outer * outer)
        out = contract(wide([columns, columns]), wide([high, low]))
        found.append((s, out[0:8] + out[8:16] + out[16:24]))
    for s, more in found:
        sums[pl.ds(pl.multiple_of(s * 16 + 8, 8), 4), :] += more[0:4]


def halo_density(ta, tb, tp, x, y, z):
    rank = lax.broadcasted_iota(jnp.int32, (4, TILE), 0)
    centre = rows(ta, a_row(x + 1, y + 1, z + 1), 4)
    support = rows(tb, b_row(x, y, z + 1), 4)[3:4]
    left, reach = own_side(centre[0:3], support)
    total = jnp.zeros((TILE, TILE), f32)
    sides = []
    for dx, dy, dz in NEIGHBOURS:
        position = rows(ta, a_row(x + 1 + dx, y + 1 + dy, z + 1 + dz), 4) + place_rows(dx, dy, dz, rank)
        eight = tall([position, jnp.zeros((4, TILE), f32)])
        sides.append((other_side(position, eight, rank), position[3:4]))
    for k, (side, mass) in enumerate(sides):
        if k % 2 == 0:
            pair = wide([side, sides[k + 1][0]]) if k + 1 < 27 else side
            both = jnp.dot(left, pair, preferred_element_type=f32)
        squares = both[:, (k % 2) * TILE : (k % 2 + 1) * TILE]
        terms = []
        for r in range(0, TILE, PIECE):
            near = reach[r : r + PIECE]
            distance = distances(squares[r : r + PIECE])
            inside = jnp.maximum(near - distance, 0.0)
            square = inside * inside
            terms.append(square * square * (distance + 0.25 * near) * mass)
        total = total + tall(terms)
    density = density_scale * lane_sums(total) / eighth_power(support)
    at = p_row(x, y, z)
    tp[pl.ds(at, 1), :] = adiabatic_less_one * tp[pl.ds(at, 1), :] / density


def mark_near(where, own, own_count, near_cells, near_counts, marks):
    brick_z = lax.broadcasted_iota(jnp.int32, (BRICK, SLOTS), 0)
    place = lax.broadcasted_iota(jnp.int32, (BRICK, SLOTS), 1)
    dz = ((brick_z - where[2] + 9) & 7) - 1
    listed = []
    for k in range(9):
        cell = near_cells[k]
        counts = [jnp.where(dz == d, near_counts[k * 3 + d + 1], 0) for d in (-1, 0, 1)]
        used = place < counts[0] + counts[1] + counts[2]
        x = (cell >> 6) + (k // 3 - 1) * BRICK
        y = ((cell >> 3) & 7) + (k % 3 - 1) * BRICK
        listed.append((jnp.where(used, x, -99), y, (cell & 7) + dz * BRICK, cell))

    def slot(s, bits):
        ox, oy, oz = slot_place(own, s)
        out = []
        for (x, y, z, _), bit in zip(listed, bits):
            far = jnp.maximum(jnp.maximum(jnp.abs(x - ox), jnp.abs(y - oy)), jnp.abs(z - oz))
            out.append(bit | jnp.where(far <= 1, jnp.left_shift(1, s), 0))
        return tuple(out)

    bits = lax.fori_loop(0, own_count, slot, (jnp.zeros((BRICK, SLOTS), jnp.int32),) * 9)
    for k in range(9):
        marks[k] = jnp.where(bits[k] == 0, 0, bits[k] | (listed[k][3] << 16))


def list_near(where, own, own_count, marks, found, found_count, pairs, pair_count):
    found_count[0] = 0
    pair_count[0] = 0

    def brick(b, carry):
        k = b // 3
        dx, dy, dz = k // 3 - 1, k % 3 - 1, b % 3 - 1
        level = (where[2] + dz) & 7

        def take(mark):
            cell = mark >> 16
            x, y, z = (cell >> 6) + dx * BRICK, ((cell >> 3) & 7) + dy * BRICK, (cell & 7) + dz * BRICK

            @pl.when(b != 13)
            def _():
                at = found_count[0]
                found[at] = near_id(x + 1, y + 1, z + 1)
                found_count[0] = at + 1

            def slot(s, carry):
                @pl.when(((mark >> s) & 1) == 1)
                def _():
                    ox, oy, oz = slot_place(own, s)
                    at = pair_count[0]
                    pairs[at] = s * 32 + (x - ox + 1) * 9 + (y - oy + 1) * 3 + z - oz + 1
                    pair_count[0] = at + 1

                return carry

            lax.fori_loop(0, own_count, slot, 0)

        for first in range(0, SLOTS, 4):
            four = [marks[k, level, first + i] for i in range(4)]

            @pl.when((four[0] | four[1] | four[2] | four[3]) != 0)
            def _():
                for mark in four:
                    pl.when(mark != 0)(functools.partial(take, mark))

        return carry

    lax.fori_loop(0, 27, brick, 0)
    for k in range(GROUP):
        pairs[pair_count[0] + k] = SLOTS * 32 + 13


def stage_needed(own, s):
    x, y, z = slot_place(own, s)
    edge = lambda v: (v == 0) | (v == BRICK - 1)
    return jnp.where(edge(y), 3, jnp.where(edge(z), 2, jnp.where(edge(x), 1, 0)))


def run_stage(stage, quota, own, count, done, body):
    def slot(s, taken):
        go = (stage_needed(own, s) <= stage) & (done[s] == 0) & (taken < quota)

        @pl.when(go)
        def _():
            body(s, (-1, 0, 1), False)
            done[s] = 1

        return taken + go.astype(jnp.int32)

    lax.fori_loop(0, count[0], slot, jnp.int32(0))


def run_edges(own, count, body, planes, more):
    def slot(s, carry):
        @pl.when(stage_needed(own, s) == 3)
        def _():
            inward = jnp.where(slot_place(own, s)[1] == 0, 1, -1)
            body(s, planes(inward), more)

        return carry

    lax.fori_loop(0, count[0], slot, 0)


def run_halo(ta, tb, tp, found, found_count, late):
    def halo(k, carry):
        cell = found[k]
        x, y, z = cell // 100, cell // 10 % 10, cell % 10
        early = (y >= 2) & (y <= 7)

        @pl.when(early != late)
        def _():
            halo_density(ta, tb, tp, x, y, z)

        return carry

    lax.fori_loop(0, found_count[0], halo, 0)


def finish_slot(own, count, ta, tb, tp, sums, s, density_out, acceleration_out, heating_out):
    used = s < count[0]
    keep = lambda value: jnp.where(used, value, 0.0)
    x, y, z = slot_place(own, s)
    centre_a = rows(ta, a_row(x + 2, y + 2, z + 2), 4)
    centre_b = rows(tb, b_row(x + 1, y + 1, z + 2), 4)
    a_sum = rows(sums, s * 16, 8, 8)
    b_sum = rows(sums, s * 16 + 8, 8, 8)
    pressure = jnp.abs(tp[pl.ds(p_row(x + 1, y + 1, z + 1), 1), :])
    own_scale = slope_scale * pressure / eighth_power(centre_b[3:4])
    moving = centre_b - jnp.mean(centre_b, axis=1, keepdims=True)
    heat = a_sum[7:8]
    inner = jnp.zeros((1, TILE), f32)
    for f in range(3):
        position, speed = centre_a[f : f + 1], moving[f : f + 1]
        inner = inner + position * speed
        heat = heat - speed * a_sum[f : f + 1] - position * a_sum[4 + f : 5 + f]
        push = own_scale * (position * a_sum[3:4] - a_sum[f : f + 1])
        push = push + slope_scale * (position * b_sum[3:4] - b_sum[f : f + 1])
        acceleration_out[f, pl.ds(s, 1), :] = keep(push)
    heating_out[pl.ds(s, 1), :] = keep(-own_scale * (heat + inner * a_sum[3:4]))
    density_out[pl.ds(s, 1), :] = keep(b_sum[7:8])


SMEM = pltpu.SMEM
VMEM = pltpu.VMEM
i32 = jnp.int32


def call(body, name, inputs, outputs, aliases=(), scratch=(), flops=0, limit=LIMIT):
    return pl.pallas_call(
        body,
        name=name,
        out_shape=[jax.ShapeDtypeStruct(shape, dtype) for shape, dtype, _ in outputs],
        in_specs=[pl.BlockSpec(memory_space=space) for _, space in inputs],
        out_specs=[pl.BlockSpec(memory_space=space) for _, _, space in outputs],
        scratch_shapes=list(scratch),
        input_output_aliases=dict(aliases),
        compiler_params=pltpu.CompilerParams(vmem_limit_bytes=limit),
        cost_estimate=pl.CostEstimate(flops=flops, bytes_accessed=1 << 20, transcendentals=0),
    )(*[array for array, _ in inputs])


def pack_x_kernel(where, cells, counts, *refs):
    pack_x(where, cells, counts, refs[:6], *refs[6:15], refs[15:21], *refs[21:])


def stage0_kernel(
    own, count, near_counts, where, near_cells, ta_in, tb_in, tp_in,
    ta, tb, tp, marks, done, lefts, reaches, supports, sums,
):
    mark_near(where, own, count[0], near_cells, near_counts, marks)
    for s in range(SLOTS):
        done[s] = 0
    prepare_slots(own, ta, tb, lefts, reaches, supports)
    body = functools.partial(slot_sums, own, ta, tb, tp, lefts, reaches, supports, sums)
    run_stage(0, QUOTAS[0], own, count, done, body)


def stage1_kernel(
    own, count, where, marks, done_in, lefts, reaches, supports, ta_in, tb_in, tp_in, sums_in,
    ta, tb, tp, done, sums, found, found_count, pairs, pair_count,
):
    list_near(where, own, count[0], marks, found, found_count, pairs, pair_count)
    for s in range(SLOTS):
        done[s] = done_in[s]
    body = functools.partial(slot_sums, own, ta, tb, tp, lefts, reaches, supports, sums)
    run_stage(1, QUOTAS[1], own, count, done, body)


def stage2_kernel(
    own, count, done_in, found, found_count, lefts, reaches, supports, ta_in, tb_in, tp_in, sums_in,
    ta, tb, tp, sums, done,
):
    for s in range(SLOTS):
        done[s] = done_in[s]
    body = functools.partial(slot_sums, own, ta, tb, tp, lefts, reaches, supports, sums)
    run_stage(2, SLOTS, own, count, done, body)
    run_edges(own, count, body, lambda inward: (0, inward), False)
    run_halo(ta, tb, tp, found, found_count, False)


def pack_kernel(fill, pack, low, high, ta_in, tb_in, tp_in, ta, tb, tp, up, down):
    fill(low, high, ta, tb, tp)
    pack(ta, tb, tp, up, down)


def last_kernel(
    own, count, found, found_count, pairs, pair_count, lefts, reaches, supports, yl, yh,
    ta_in, tb_in, tp_in, sums_in, density_out, acceleration_out, heating_out, ta, tb, tp, sums,
):
    fill_y(yl, yh, ta, tb, tp)
    body = functools.partial(slot_sums, own, ta, tb, tp, lefts, reaches, supports, sums)
    run_edges(own, count, body, lambda inward: (-inward,), True)
    run_halo(ta, tb, tp, found, found_count, True)

    def renew(g, carry):
        for s in (g * 4, g * 4 + 1, g * 4 + 2, g * 4 + 3):
            x, y, z = slot_place(own, s)
            at = p_row(x + 1, y + 1, z + 1)
            support = rows(tb, b_row(x + 1, y + 1, z + 2), 4)[3:4]
            density = density_scale * sums[pl.ds(s * 16 + 15, 1), :] / eighth_power(support)
            sums[pl.ds(s * 16 + 15, 1), :] = density
            tp[pl.ds(at, 1), :] = adiabatic_less_one * tp[pl.ds(at, 1), :] / density
        return carry

    lax.fori_loop(0, SLOTS // 4, renew, 0)

    def some_pairs(g, carry):
        active_pairs(pairs, own, ta, tb, tp, lefts, sums, g * GROUP, GROUP)
        return carry

    lax.fori_loop(0, (pair_count[0] + GROUP - 1) // GROUP, some_pairs, 0)

    def finish(g, carry):
        for s in (g * 4, g * 4 + 1, g * 4 + 2, g * 4 + 3):
            finish_slot(own, count, ta, tb, tp, sums, s, density_out, acceleration_out, heating_out)
        return carry

    lax.fori_loop(0, SLOTS // 4, finish, 0)


QUOTAS = (3, 5)


def shift_both(axis, up, down):
    devices = lax.axis_size(axis)
    higher = [(i, (i + 1) % devices) for i in range(devices)]
    lower = [(j, i) for i, j in higher]
    return lax.ppermute(up, axis, higher), lax.ppermute(down, axis, lower)


def on_device(offsets, velocity, mass, support, energy, old_density, active_cells, active_count):
    where = jnp.stack([lax.axis_index(a) for a in ("gx", "gy", "gz")]).astype(i32)
    grow = lambda n: ((n, TILE), f32, VMEM)
    tables = [grow(A_ROWS), grow(B_ROWS), grow(P_ROWS)]
    fields = [offsets, velocity, mass, support, energy, old_density]
    stay = lambda array: pltpu.with_memory_space_constraint(array, pltpu.HBM)
    fields = [stay(field) for field in fields]
    scalars = lambda n: ((n,), i32, SMEM)
    near_shape = ((9, BRICK, SLOTS), i32, VMEM)
    own, count, near_counts, near_cells, ta, tb, tp, up, down = call(
        pack_x_kernel, "pack_x",
        [(where, SMEM), (stay(active_cells), pltpu.HBM), (stay(active_count), pltpu.HBM)] + [(f, pltpu.HBM) for f in fields],
        [scalars(SLOTS), scalars(1), scalars(27), near_shape, *tables, grow(X_ROWS), grow(X_ROWS)],
        scratch=[VMEM(f.shape, f32) for f in fields]
        + [SMEM((3, BRICK, BRICK), i32), SMEM((BRICK, SLOTS), i32), pltpu.SemaphoreType.DMA((19,))],
    )
    xl, xh = shift_both("gx", up, down)
    slot_tables = [((SLOTS, TILE, 48), bf16, VMEM), ((SLOTS, TILE, TILE), f32, VMEM), ((SLOTS, TILE, TILE), f32, VMEM)]
    sums_shape = grow((SLOTS + 1) * 16)
    ta, tb, tp, marks, done, lefts, reaches, supports, sums = call(
        stage0_kernel, "stage0",
        [(own, SMEM), (count, SMEM), (near_counts, SMEM), (where, SMEM)]
        + [(near_cells, VMEM), (ta, VMEM), (tb, VMEM), (tp, VMEM)],
        [*tables, near_shape, scalars(SLOTS), *slot_tables, sums_shape],
        {5: 0, 6: 1, 7: 2}, flops=8_000_000_000,
    )

    def packed(fill, pack, name, low, high, ta, tb, tp, length):
        return call(
            functools.partial(pack_kernel, fill, pack), name, [(v, VMEM) for v in (low, high, ta, tb, tp)],
            [*tables, grow(length), grow(length)], {2: 0, 3: 1, 4: 2},
        )

    ta, tb, tp, up, down = packed(fill_x, pack_z, "pack_z", xl, xh, ta, tb, tp, Z_ROWS)
    zl, zh = shift_both("gz", up, down)
    ta, tb, tp, done, sums, *lists = call(
        stage1_kernel, "stage1",
        [(v, SMEM) for v in (own, count, where, marks, done)]
        + [(v, VMEM) for v in (lefts, reaches, supports, ta, tb, tp, sums)],
        [*tables, scalars(SLOTS), sums_shape, scalars(512), scalars(1), scalars(PAIRS), scalars(1)],
        {8: 0, 9: 1, 10: 2, 11: 4}, flops=8_000_000_000,
    )
    ta, tb, tp, up, down = packed(fill_z, pack_y, "pack_y", zl, zh, ta, tb, tp, Y_ROWS)
    yl, yh = shift_both("gy", up, down)
    ta, tb, tp, sums = call(
        stage2_kernel, "stage2",
        [(v, SMEM) for v in (own, count, done, *lists[:2])]
        + [(v, VMEM) for v in (lefts, reaches, supports, ta, tb, tp, sums)],
        [*tables, sums_shape], {8: 0, 9: 1, 10: 2, 11: 3}, scratch=[SMEM((SLOTS,), i32)], flops=8_000_000_000,
    )
    density, acceleration, heating, *_ = call(
        last_kernel, "last",
        [(v, SMEM) for v in (own, count, *lists)]
        + [(v, VMEM) for v in (lefts, reaches, supports, yl, yh, ta, tb, tp, sums)],
        [((SLOTS, TILE), f32, VMEM), ((3, SLOTS, TILE), f32, VMEM), ((SLOTS, TILE), f32, VMEM), *tables, sums_shape],
        {11: 3, 12: 4, 13: 5, 14: 6}, flops=1_000_000_000,
    )
    shape_out = (1, 1, 1, SLOTS, TILE)
    return density.reshape(shape_out), acceleration.reshape((3,) + shape_out), heating.reshape(shape_out)


def solution(mesh):
    in_specs = (
        P(None, "gx", "gy", "gz", None),
        P(None, "gx", "gy", "gz", None),
        P("gx", "gy", "gz", None),
        P("gx", "gy", "gz", None),
        P("gx", "gy", "gz", None),
        P("gx", "gy", "gz", None),
        P(),
        P(),
    )
    out_specs = (
        P("gx", "gy", "gz", None, None),
        P(None, "gx", "gy", "gz", None, None),
        P("gx", "gy", "gz", None, None),
    )
    return jax.shard_map(
        on_device, mesh=mesh, in_specs=in_specs, out_specs=out_specs, check_vma=False
    )
```

```python
import functools
import math

import jax
import jax.numpy as jnp
from jax import lax
from jax.experimental import pallas as pl
from jax.experimental.pallas import tpu as pltpu
from jax.sharding import PartitionSpec as P

BRICK = 8
WIDE = BRICK + 4
NEAR = BRICK + 2
ROW = 16
SLOTS = 16
TILE = 128
A_ROWS = WIDE * WIDE * WIDE * 4
B_ROWS = NEAR * NEAR * WIDE * 4
P_ROWS = NEAR * NEAR * ROW
X_ROWS = 2 * 64 * 4 + 64 * 4 + 64
Z_ROWS = 96 * 8 + 80 * 4 + 80
Y_ROWS = 12 * 96 + 10 * 48 + 10 * 16
PAIRS = 512
GROUP = 8
LIMIT = 16 * 1024 * 1024

adiabatic_less_one = 2.0 / 3.0
kernel_norm = 21.0 / (2.0 * math.pi)
density_scale = kernel_norm / (256.0 * TILE)
slope_scale = 20.0 * kernel_norm / (64.0 * TILE)
TINY = 1e-30

bf16 = jnp.bfloat16
f32 = jnp.float32


def a_row(x, y, z):
    return ((x * WIDE + y) * WIDE + z) * 4


def b_row(x, y, z):
    return ((x * NEAR + y) * WIDE + z) * 4


def p_row(x, y, z):
    return (x * NEAR + y) * ROW + ((z + 7) & 15)


def near_id(x, y, z):
    return (x * NEAR + y) * NEAR + z


def rows(ref, start, size, multiple=4):
    return ref[pl.ds(pl.multiple_of(start, multiple), size), :]


def put(ref, start, value, multiple=4):
    ref[pl.ds(pl.multiple_of(start, multiple), value.shape[0]), :] = value


def move(to, to_row, source, row, size):
    to[to_row : to_row + size, :] = source[row : row + size, :]


def pack_x(
    where, cells, counts, fields, own, count, near_counts, near_cells, ta, tb, tp, up, down, held, count_tiles, own_tile, sems
):
    copies = [pltpu.make_async_copy(field, place, sems.at[k]) for k, (field, place) in enumerate(zip(fields, held))]
    for copy in copies:
        copy.start()
    lists = []
    for k in range(9):
        a, b = (where[0] + k // 3 - 1) & 7, (where[1] + k % 3 - 1) & 7
        lists.append(pltpu.make_async_copy(cells.at[a, b], near_cells.at[k], sems.at[6 + k]))
        if k % 3 == 0:
            lists.append(pltpu.make_async_copy(counts.at[a], count_tiles.at[k // 3], sems.at[15 + k // 3]))
    own_copy = pltpu.make_async_copy(cells.at[where[0], where[1]], own_tile, sems.at[18])
    lists.append(own_copy)
    for copy in lists:
        copy.start()
    for copy in lists:
        copy.wait()
    for s in range(SLOTS):
        own[s] = own_tile[where[2], s]
    for k in range(27):
        b, d = (where[1] + k // 3 % 3 - 1) & 7, (where[2] + k % 3 - 1) & 7
        near_counts[k] = count_tiles[k // 9, b, d]
    count[0] = near_counts[13]
    for copy in copies:
        copy.wait()
    off, vel, mass, sup, energy, old = held
    for x in range(BRICK):
        for y in range(BRICK):
            a, b = a_row(x + 2, y + 2, 2), b_row(x + 1, y + 1, 2)
            for f in range(3):
                ta[pl.ds(a + f, BRICK, stride=4), :] = off[f, x, y] - 0.5
                tb[pl.ds(b + f, BRICK, stride=4), :] = vel[f, x, y]
            ta[pl.ds(a + 3, BRICK, stride=4), :] = mass[x, y]
            tb[pl.ds(b + 3, BRICK, stride=4), :] = sup[x, y]
            p = p_row(x + 1, y + 1, 1)
            tp[p : p + BRICK, :] = adiabatic_less_one * energy[x, y] / old[x, y]

    def slot(s, carry):
        x, y, z = slot_place(own, s)
        tp[pl.ds(p_row(x + 1, y + 1, z + 1), 1), :] = -energy[x, y, pl.ds(z, 1), :]
        return carry

    lax.fori_loop(0, count[0], slot, 0)
    for ref, xa, xb in ((up, 8, 8), (down, 2, 1)):
        for y in range(BRICK):
            for layer in range(2):
                move(ref, (layer * 8 + y) * 32, ta, a_row(xa + layer, y + 2, 2), 32)
            move(ref, 512 + y * 32, tb, b_row(xb, y + 1, 2), 32)
            move(ref, 768 + y * 8, tp, p_row(xb, y + 1, 1), 8)


def fill_x(low, high, ta, tb, tp):
    for ref, xa, xb in ((low, 0, 0), (high, 10, 9)):
        for y in range(BRICK):
            for layer in range(2):
                move(ta, a_row(xa + layer, y + 2, 2), ref, (layer * 8 + y) * 32, 32)
            move(tb, b_row(xb, y + 1, 2), ref, 512 + y * 32, 32)
            move(tp, p_row(xb, y + 1, 1), ref, 768 + y * 8, 8)


def pack_z(ta, tb, tp, up, down):
    for ref, za, zb, zp in ((up, 8, 9, 8), (down, 2, 2, 1)):
        for i in range(96):
            move(ref, i * 8, ta, a_row(i // 8, i % 8 + 2, za), 8)
        for i in range(80):
            move(ref, 768 + i * 4, tb, b_row(i // 8, i % 8 + 1, zb), 4)
            move(ref, 1088 + i, tp, p_row(i // 8, i % 8 + 1, zp), 1)


def fill_z(low, high, ta, tb, tp):
    for ref, za, zb, zp in ((low, 0, 1, 0), (high, 10, 10, 9)):
        for i in range(96):
            move(ta, a_row(i // 8, i % 8 + 2, za), ref, i * 8, 8)
        for i in range(80):
            move(tb, b_row(i // 8, i % 8 + 1, zb), ref, 768 + i * 4, 4)
            move(tp, p_row(i // 8, i % 8 + 1, zp), ref, 1088 + i, 1)


def pack_y(ta, tb, tp, up, down):
    for ref, ya, yb in ((up, 8, 8), (down, 2, 1)):
        for x in range(WIDE):
            move(ref, x * 96, ta, a_row(x, ya, 0), 96)
        for x in range(NEAR):
            move(ref, 1152 + x * 48, tb, b_row(x, yb, 0), 48)
            move(ref, 1632 + x * 16, tp, (x * NEAR + yb) * ROW, 16)


def fill_y(low, high, ta, tb, tp):
    for ref, ya, yb in ((low, 0, 0), (high, 10, 9)):
        for x in range(WIDE):
            move(ta, a_row(x, ya, 0), ref, x * 96, 96)
        for x in range(NEAR):
            move(tb, b_row(x, yb, 0), ref, 1152 + x * 48, 48)
            move(tp, (x * NEAR + yb) * ROW, ref, 1632 + x * 16, 16)


def thirds(value):
    high = value.astype(bf16).astype(f32)
    rest = value - high
    middle = rest.astype(bf16).astype(f32)
    return high, middle, rest - middle


def own_side(position, support):
    x, y, z = position[0:1], position[1:2], position[2:3]
    square = x * x + y * y + z * z
    zero = jnp.zeros((3, TILE), f32)
    eight = jnp.concatenate(
        [-32.0 * x, -32.0 * y, -32.0 * z, jnp.full((1, TILE), 16.0, f32), 16.0 * square, zero], axis=0
    )
    first, second, third = thirds(eight)
    four = jnp.concatenate([4.0 * support, jnp.zeros((7, TILE), f32)], axis=0)
    filler = jnp.zeros((TILE - 56, TILE), f32)
    stacked = jnp.concatenate([first, first, first, second, second, third, four, filler], axis=0)
    turned = stacked.T
    reach = jnp.broadcast_to(turned[:, 48:49], (TILE, TILE))
    return turned[:, 0:48].astype(bf16), reach


def distances(square):
    square = jnp.maximum(square, TINY)
    return square * lax.rsqrt(square)


def halves(value):
    high = value.astype(bf16)
    return high, (value - high.astype(f32)).astype(bf16)


def contract(columns, weights):
    return lax.dot_general(columns, weights, (((1,), (1,)), ((), ())), preferred_element_type=f32)


def wide(parts):
    return jnp.concatenate(parts, axis=1)


def tall(parts):
    return jnp.concatenate(parts, axis=0)


def eighth_power(value):
    value = value * value
    value = value * value
    return value * value


def slot_place(own, s):
    cell = own[s]
    return cell >> 6, (cell >> 3) & 7, cell & 7


def lane_sums(value):
    return jnp.sum(value.T, axis=0, keepdims=True)


def place_rows(dx, dy, dz, rank):
    fx, fy, fz = (jnp.asarray(d).astype(f32) for d in (dx, dy, dz))
    return jnp.where(rank == 0, fx, jnp.where(rank == 1, fy, jnp.where(rank == 2, fz, 0.0)))


def other_side(position, eight, rank):
    square = jnp.sum(jnp.where(rank < 3, position * position, 0.0), axis=0, keepdims=True)
    line = lax.broadcasted_iota(jnp.int32, (8, TILE), 0)
    mixed = jnp.where(line < 3, eight, jnp.where(line == 3, square, jnp.where(line == 4, 1.0, 0.0)))
    first, second, third = thirds(mixed)
    return tall([first, second, third, first, second, first]).astype(bf16)


def weigh(weight, base):
    return tall(thirds(weight * base)).astype(bf16)


NEIGHBOURS = [(dx, dy, dz) for dx in (-1, 0, 1) for dy in (-1, 0, 1) for dz in (-1, 0, 1)]
PIECE = 32


def prepare_slots(own, ta, tb, lefts, reaches, supports):
    def group(g, carry):
        for k in range(4):
            s = g * 4 + k
            x, y, z = slot_place(own, s)
            position = rows(ta, a_row(x + 2, y + 2, z + 2), 4)
            support = rows(tb, b_row(x + 1, y + 1, z + 2), 4)[3:4]
            left, reach = own_side(position[0:3], support)
            lefts[s] = left
            reaches[s] = reach
            supports[s] = 0.25 * reach
        return carry

    lax.fori_loop(0, SLOTS // 4, group, 0)


def slot_sums(own, ta, tb, tp, lefts, reaches, supports, sums, s, planes, more):
    x, y, z = slot_place(own, s)
    rank = lax.broadcasted_iota(jnp.int32, (4, TILE), 0)
    line = lax.broadcasted_iota(jnp.int32, (8, TILE), 0)
    centre = rows(tb, b_row(x + 1, y + 1, z + 2), 4)
    drift = jnp.where(rank < 3, jnp.mean(centre, axis=1, keepdims=True), 0.0)
    left = lefts[s]
    total = jnp.zeros((TILE, TILE), f32)
    a_columns, b_columns, a_weights, b_weights, sides = [], [], [], [], []
    for dx, dy, dz in [(dx, dy, dz) for dy in planes for dx in (-1, 0, 1) for dz in (-1, 0, 1)]:
        position = rows(ta, a_row(x + 2 + dx, y + 2 + dy, z + 2 + dz), 4) + place_rows(dx, dy, dz, rank)
        motion = rows(tb, b_row(x + 1 + dx, y + 1 + dy, z + 2 + dz), 4) - drift
        mass, support = position[3:4], motion[3:4]
        pressure = tp[pl.ds(p_row(x + 1 + dx, y + 1 + dy, z + 1 + dz), 1), :]
        still = jnp.maximum(pressure, 0.0)
        inner = jnp.sum(jnp.where(rank < 3, position * motion, 0.0), axis=0, keepdims=True)
        eight = tall([position, motion])
        base = jnp.where(line == 3, 1.0, jnp.where(line == 7, inner, eight))
        a_columns += [weigh(mass, base)] * 2
        b_columns += [weigh(mass * still / eighth_power(support), base)] * 2
        sides.append((other_side(position, eight, rank), mass, 4.0 * support))
    for k, (side, mass, support) in enumerate(sides):
        if k % 2 == 0:
            pair = wide([side, sides[k + 1][0]]) if k + 1 < len(sides) else side
            both = jnp.dot(left, pair, preferred_element_type=f32)
        squares = both[:, (k % 2) * TILE : (k % 2 + 1) * TILE]
        terms, a_high, a_low, b_high, b_low = [], [], [], [], []
        for r in range(0, TILE, PIECE):
            reach = reaches[s, r : r + PIECE, :]
            distance = distances(squares[r : r + PIECE])
            inside = jnp.maximum(reach - distance, 0.0)
            square = inside * inside
            terms.append(square * square * (distance + supports[s, r : r + PIECE, :]) * mass)
            high, low = halves(square * inside)
            a_high.append(high)
            a_low.append(low)
            outer = jnp.maximum(support - distance, 0.0)
            high, low = halves(outer * outer * outer)
            b_high.append(high)
            b_low.append(low)
        total = total + tall(terms)
        a_weights += [tall(a_high), tall(a_low)]
        b_weights += [tall(b_high), tall(b_low)]
    a_sum = contract(wide(a_columns), wide(a_weights))
    b_sum = contract(wide(b_columns), wide(b_weights))
    at = s * 16
    a_sum = a_sum[0:8] + a_sum[8:16] + a_sum[16:24]
    b_sum = jnp.where(line == 7, lane_sums(total), b_sum[0:8] + b_sum[8:16] + b_sum[16:24])
    if more:
        a_sum = a_sum + rows(sums, at, 8, 8)
        b_sum = b_sum + rows(sums, at + 8, 8, 8)
    put(sums, at, a_sum, 8)
    put(sums, at + 8, b_sum, 8)


def active_pairs(pairs, own, ta, tb, tp, lefts, sums, first, size):
    rank = lax.broadcasted_iota(jnp.int32, (4, TILE), 0)
    line = lax.broadcasted_iota(jnp.int32, (8, TILE), 0)
    found = []
    for k in range(size):
        pair = pairs[first + k]
        s, n = pair >> 5, pair & 31
        x, y, z = slot_place(own, s & 15)
        dx, dy, dz = n // 9 - 1, n // 3 % 3 - 1, n % 3 - 1
        position = rows(ta, a_row(x + 2 + dx, y + 2 + dy, z + 2 + dz), 4) + place_rows(dx, dy, dz, rank)
        support = rows(tb, b_row(x + 1 + dx, y + 1 + dy, z + 2 + dz), 4)[3:4]
        pressure = jnp.abs(tp[pl.ds(p_row(x + 1 + dx, y + 1 + dy, z + 1 + dz), 1), :])
        eight = tall([position, jnp.zeros((4, TILE), f32)])
        base = jnp.where(line == 3, 1.0, jnp.where(line < 3, eight, 0.0))
        columns = weigh(position[3:4] * pressure / eighth_power(support), base)
        squares = jnp.dot(lefts[s & 15], other_side(position, eight, rank), preferred_element_type=f32)
        outer = jnp.maximum(4.0 * support - distances(squares), 0.0)
        high, low = halves(outer * outer * outer)
        out = contract(wide([columns, columns]), wide([high, low]))
        found.append((s, out[0:8] + out[8:16] + out[16:24]))
    for s, more in found:
        sums[pl.ds(pl.multiple_of(s * 16 + 8, 8), 4), :] += more[0:4]


def halo_density(ta, tb, tp, x, y, z):
    rank = lax.broadcasted_iota(jnp.int32, (4, TILE), 0)
    centre = rows(ta, a_row(x + 1, y + 1, z + 1), 4)
    support = rows(tb, b_row(x, y, z + 1), 4)[3:4]
    left, reach = own_side(centre[0:3], support)
    total = jnp.zeros((TILE, TILE), f32)
    sides = []
    for dx, dy, dz in NEIGHBOURS:
        position = rows(ta, a_row(x + 1 + dx, y + 1 + dy, z + 1 + dz), 4) + place_rows(dx, dy, dz, rank)
        eight = tall([position, jnp.zeros((4, TILE), f32)])
        sides.append((other_side(position, eight, rank), position[3:4]))
    for k, (side, mass) in enumerate(sides):
        if k % 2 == 0:
            pair = wide([side, sides[k + 1][0]]) if k + 1 < 27 else side
            both = jnp.dot(left, pair, preferred_element_type=f32)
        squares = both[:, (k % 2) * TILE : (k % 2 + 1) * TILE]
        terms = []
        for r in range(0, TILE, PIECE):
            near = reach[r : r + PIECE]
            distance = distances(squares[r : r + PIECE])
            inside = jnp.maximum(near - distance, 0.0)
            square = inside * inside
            terms.append(square * square * (distance + 0.25 * near) * mass)
        total = total + tall(terms)
    density = density_scale * lane_sums(total) / eighth_power(support)
    at = p_row(x, y, z)
    tp[pl.ds(at, 1), :] = adiabatic_less_one * tp[pl.ds(at, 1), :] / density


def mark_near(where, own, own_count, near_cells, near_counts, marks):
    brick_z = lax.broadcasted_iota(jnp.int32, (BRICK, SLOTS), 0)
    place = lax.broadcasted_iota(jnp.int32, (BRICK, SLOTS), 1)
    dz = ((brick_z - where[2] + 9) & 7) - 1
    listed = []
    for k in range(9):
        cell = near_cells[k]
        counts = [jnp.where(dz == d, near_counts[k * 3 + d + 1], 0) for d in (-1, 0, 1)]
        used = place < counts[0] + counts[1] + counts[2]
        x = (cell >> 6) + (k // 3 - 1) * BRICK
        y = ((cell >> 3) & 7) + (k % 3 - 1) * BRICK
        listed.append((jnp.where(used, x, -99), y, (cell & 7) + dz * BRICK, cell))

    def slot(s, bits):
        ox, oy, oz = slot_place(own, s)
        out = []
        for (x, y, z, _), bit in zip(listed, bits):
            far = jnp.maximum(jnp.maximum(jnp.abs(x - ox), jnp.abs(y - oy)), jnp.abs(z - oz))
            out.append(bit | jnp.where(far == 1, jnp.left_shift(1, s), 0))
        return tuple(out)

    bits = lax.fori_loop(0, own_count, slot, (jnp.zeros((BRICK, SLOTS), jnp.int32),) * 9)
    for k in range(9):
        marks[k] = jnp.where(bits[k] == 0, 0, bits[k] | (listed[k][3] << 16))
        places = jnp.where(bits[k] == 0, 0, jnp.left_shift(1, place)).astype(f32)
        whole = jnp.sum(places, axis=1, keepdims=True).astype(jnp.int32)
        marks[9 + k] = jnp.broadcast_to(whole, (BRICK, SLOTS))


def list_near(where, own, own_count, marks, found, found_count, pairs, pair_count):
    found_count[0] = 0

    def itself(s, carry):
        pairs[s] = s * 32 + 13
        return carry

    lax.fori_loop(0, own_count, itself, 0)
    pair_count[0] = own_count

    def brick(b, carry):
        k = b // 3
        dx, dy, dz = k // 3 - 1, k % 3 - 1, b % 3 - 1
        level = (where[2] + dz) & 7
        places = marks[9 + k, level, 0]

        def listed(i, carry):
            @pl.when(((places >> i) & 1) == 1)
            def _():
                mark = marks[k, level, i]
                cell = mark >> 16
                x, y, z = (cell >> 6) + dx * BRICK, ((cell >> 3) & 7) + dy * BRICK, (cell & 7) + dz * BRICK

                @pl.when(b != 13)
                def _():
                    at = found_count[0]
                    found[at] = near_id(x + 1, y + 1, z + 1)
                    found_count[0] = at + 1

                def slot(s, carry):
                    @pl.when(((mark >> s) & 1) == 1)
                    def _():
                        ox, oy, oz = slot_place(own, s)
                        at = pair_count[0]
                        pairs[at] = s * 32 + (x - ox + 1) * 9 + (y - oy + 1) * 3 + z - oz + 1
                        pair_count[0] = at + 1

                    return carry

                lax.fori_loop(0, own_count, slot, 0)

            return carry

        @pl.when(places != 0)
        def _():
            lax.fori_loop(0, SLOTS, listed, 0)

        return carry

    lax.fori_loop(0, 27, brick, 0)
    for k in range(GROUP):
        pairs[pair_count[0] + k] = SLOTS * 32 + 13


def stage_needed(own, s):
    x, y, z = slot_place(own, s)
    edge = lambda v: (v == 0) | (v == BRICK - 1)
    return jnp.where(edge(y), 3, jnp.where(edge(z), 2, jnp.where(edge(x), 1, 0)))


def run_stage(stage, quota, own, count, done, body):
    def slot(s, taken):
        go = (stage_needed(own, s) <= stage) & (done[s] == 0) & (taken < quota)

        @pl.when(go)
        def _():
            body(s, (-1, 0, 1), False)
            done[s] = 1

        return taken + go.astype(jnp.int32)

    lax.fori_loop(0, count[0], slot, jnp.int32(0))


def run_edges(own, count, body, planes, more):
    def slot(s, carry):
        @pl.when(stage_needed(own, s) == 3)
        def _():
            inward = jnp.where(slot_place(own, s)[1] == 0, 1, -1)
            body(s, planes(inward), more)

        return carry

    lax.fori_loop(0, count[0], slot, 0)


def run_halo(ta, tb, tp, found, found_count, late):
    def halo(k, carry):
        cell = found[k]
        x, y, z = cell // 100, cell // 10 % 10, cell % 10
        early = (y >= 2) & (y <= 7)

        @pl.when(early != late)
        def _():
            halo_density(ta, tb, tp, x, y, z)

        return carry

    lax.fori_loop(0, found_count[0], halo, 0)


def finish_slot(own, count, ta, tb, tp, sums, s, density_out, acceleration_out, heating_out):
    used = s < count[0]
    keep = lambda value: jnp.where(used, value, 0.0)
    x, y, z = slot_place(own, s)
    centre_a = rows(ta, a_row(x + 2, y + 2, z + 2), 4)
    centre_b = rows(tb, b_row(x + 1, y + 1, z + 2), 4)
    a_sum = rows(sums, s * 16, 8, 8)
    b_sum = rows(sums, s * 16 + 8, 8, 8)
    pressure = jnp.abs(tp[pl.ds(p_row(x + 1, y + 1, z + 1), 1), :])
    own_scale = slope_scale * pressure / eighth_power(centre_b[3:4])
    moving = centre_b - jnp.mean(centre_b, axis=1, keepdims=True)
    heat = a_sum[7:8]
    inner = jnp.zeros((1, TILE), f32)
    for f in range(3):
        position, speed = centre_a[f : f + 1], moving[f : f + 1]
        inner = inner + position * speed
        heat = heat - speed * a_sum[f : f + 1] - position * a_sum[4 + f : 5 + f]
        push = own_scale * (position * a_sum[3:4] - a_sum[f : f + 1])
        push = push + slope_scale * (position * b_sum[3:4] - b_sum[f : f + 1])
        acceleration_out[f, pl.ds(s, 1), :] = keep(push)
    heating_out[pl.ds(s, 1), :] = keep(-own_scale * (heat + inner * a_sum[3:4]))
    density_out[pl.ds(s, 1), :] = keep(b_sum[7:8])


SMEM = pltpu.SMEM
VMEM = pltpu.VMEM
i32 = jnp.int32


def call(body, name, inputs, outputs, aliases=(), scratch=(), flops=0, limit=LIMIT):
    return pl.pallas_call(
        body,
        name=name,
        out_shape=[jax.ShapeDtypeStruct(shape, dtype) for shape, dtype, _ in outputs],
        in_specs=[pl.BlockSpec(memory_space=space) for _, space in inputs],
        out_specs=[pl.BlockSpec(memory_space=space) for _, _, space in outputs],
        scratch_shapes=list(scratch),
        input_output_aliases=dict(aliases),
        compiler_params=pltpu.CompilerParams(vmem_limit_bytes=limit),
        cost_estimate=pl.CostEstimate(flops=flops, bytes_accessed=1 << 20, transcendentals=0),
    )(*[array for array, _ in inputs])


def pack_x_kernel(where, cells, counts, *refs):
    pack_x(where, cells, counts, refs[:6], *refs[6:15], refs[15:21], *refs[21:])


def stage0_kernel(
    own, count, near_counts, where, near_cells, ta_in, tb_in, tp_in,
    ta, tb, tp, marks, done, lefts, reaches, supports, sums,
):
    mark_near(where, own, count[0], near_cells, near_counts, marks)
    for s in range(SLOTS):
        done[s] = 0
    prepare_slots(own, ta, tb, lefts, reaches, supports)
    body = functools.partial(slot_sums, own, ta, tb, tp, lefts, reaches, supports, sums)
    run_stage(0, QUOTAS[0], own, count, done, body)


def stage1_kernel(
    own, count, where, marks, done_in, lefts, reaches, supports, ta_in, tb_in, tp_in, sums_in,
    ta, tb, tp, done, sums, found, found_count, pairs, pair_count,
):
    list_near(where, own, count[0], marks, found, found_count, pairs, pair_count)
    for s in range(SLOTS):
        done[s] = done_in[s]
    body = functools.partial(slot_sums, own, ta, tb, tp, lefts, reaches, supports, sums)
    run_stage(1, QUOTAS[1], own, count, done, body)


def stage2_kernel(
    own, count, done_in, found, found_count, lefts, reaches, supports, ta_in, tb_in, tp_in, sums_in,
    ta, tb, tp, sums, done,
):
    for s in range(SLOTS):
        done[s] = done_in[s]
    body = functools.partial(slot_sums, own, ta, tb, tp, lefts, reaches, supports, sums)
    run_stage(2, SLOTS, own, count, done, body)
    run_edges(own, count, body, lambda inward: (0, inward), False)
    run_halo(ta, tb, tp, found, found_count, False)


def pack_kernel(fill, pack, low, high, ta_in, tb_in, tp_in, ta, tb, tp, up, down):
    fill(low, high, ta, tb, tp)
    pack(ta, tb, tp, up, down)


def last_kernel(
    own, count, found, found_count, pairs, pair_count, lefts, reaches, supports, yl, yh,
    ta_in, tb_in, tp_in, sums_in, density_out, acceleration_out, heating_out, ta, tb, tp, sums,
):
    fill_y(yl, yh, ta, tb, tp)
    body = functools.partial(slot_sums, own, ta, tb, tp, lefts, reaches, supports, sums)
    run_edges(own, count, body, lambda inward: (-inward,), True)
    run_halo(ta, tb, tp, found, found_count, True)

    def renew(g, carry):
        for s in (g * 4, g * 4 + 1, g * 4 + 2, g * 4 + 3):
            x, y, z = slot_place(own, s)
            at = p_row(x + 1, y + 1, z + 1)
            support = rows(tb, b_row(x + 1, y + 1, z + 2), 4)[3:4]
            density = density_scale * sums[pl.ds(s * 16 + 15, 1), :] / eighth_power(support)
            sums[pl.ds(s * 16 + 15, 1), :] = density
            tp[pl.ds(at, 1), :] = adiabatic_less_one * tp[pl.ds(at, 1), :] / density
        return carry

    lax.fori_loop(0, SLOTS // 4, renew, 0)

    def some_pairs(g, carry):
        active_pairs(pairs, own, ta, tb, tp, lefts, sums, g * GROUP, GROUP)
        return carry

    lax.fori_loop(0, (pair_count[0] + GROUP - 1) // GROUP, some_pairs, 0)

    def finish(g, carry):
        for s in (g * 4, g * 4 + 1, g * 4 + 2, g * 4 + 3):
            finish_slot(own, count, ta, tb, tp, sums, s, density_out, acceleration_out, heating_out)
        return carry

    lax.fori_loop(0, SLOTS // 4, finish, 0)


QUOTAS = (3, 4)


def shift_both(axis, up, down):
    devices = lax.axis_size(axis)
    higher = [(i, (i + 1) % devices) for i in range(devices)]
    lower = [(j, i) for i, j in higher]
    return lax.ppermute(up, axis, higher), lax.ppermute(down, axis, lower)


def on_device(offsets, velocity, mass, support, energy, old_density, active_cells, active_count):
    where = jnp.stack([lax.axis_index(a) for a in ("gx", "gy", "gz")]).astype(i32)
    grow = lambda n: ((n, TILE), f32, VMEM)
    tables = [grow(A_ROWS), grow(B_ROWS), grow(P_ROWS)]
    fields = [offsets, velocity, mass, support, energy, old_density]
    stay = lambda array: pltpu.with_memory_space_constraint(array, pltpu.HBM)
    fields = [stay(field) for field in fields]
    scalars = lambda n: ((n,), i32, SMEM)
    near_shape = ((9, BRICK, SLOTS), i32, VMEM)
    own, count, near_counts, near_cells, ta, tb, tp, up, down = call(
        pack_x_kernel, "pack_x",
        [(where, SMEM), (stay(active_cells), pltpu.HBM), (stay(active_count), pltpu.HBM)] + [(f, pltpu.HBM) for f in fields],
        [scalars(SLOTS), scalars(1), scalars(27), near_shape, *tables, grow(X_ROWS), grow(X_ROWS)],
        scratch=[VMEM(f.shape, f32) for f in fields]
        + [SMEM((3, BRICK, BRICK), i32), SMEM((BRICK, SLOTS), i32), pltpu.SemaphoreType.DMA((19,))],
    )
    xl, xh = shift_both("gx", up, down)
    slot_tables = [((SLOTS, TILE, 48), bf16, VMEM), ((SLOTS, TILE, TILE), f32, VMEM), ((SLOTS, TILE, TILE), f32, VMEM)]
    sums_shape = grow((SLOTS + 1) * 16)
    ta, tb, tp, marks, done, lefts, reaches, supports, sums = call(
        stage0_kernel, "stage0",
        [(own, SMEM), (count, SMEM), (near_counts, SMEM), (where, SMEM)]
        + [(near_cells, VMEM), (ta, VMEM), (tb, VMEM), (tp, VMEM)],
        [*tables, ((18, BRICK, SLOTS), i32, VMEM), scalars(SLOTS), *slot_tables, sums_shape],
        {5: 0, 6: 1, 7: 2}, flops=8_000_000_000,
    )

    def packed(fill, pack, name, low, high, ta, tb, tp, length):
        return call(
            functools.partial(pack_kernel, fill, pack), name, [(v, VMEM) for v in (low, high, ta, tb, tp)],
            [*tables, grow(length), grow(length)], {2: 0, 3: 1, 4: 2},
        )

    ta, tb, tp, up, down = packed(fill_x, pack_z, "pack_z", xl, xh, ta, tb, tp, Z_ROWS)
    zl, zh = shift_both("gz", up, down)
    ta, tb, tp, done, sums, *lists = call(
        stage1_kernel, "stage1",
        [(v, SMEM) for v in (own, count, where, marks, done)]
        + [(v, VMEM) for v in (lefts, reaches, supports, ta, tb, tp, sums)],
        [*tables, scalars(SLOTS), sums_shape, scalars(512), scalars(1), scalars(PAIRS), scalars(1)],
        {8: 0, 9: 1, 10: 2, 11: 4}, flops=8_000_000_000,
    )
    ta, tb, tp, up, down = packed(fill_z, pack_y, "pack_y", zl, zh, ta, tb, tp, Y_ROWS)
    yl, yh = shift_both("gy", up, down)
    ta, tb, tp, sums = call(
        stage2_kernel, "stage2",
        [(v, SMEM) for v in (own, count, done, *lists[:2])]
        + [(v, VMEM) for v in (lefts, reaches, supports, ta, tb, tp, sums)],
        [*tables, sums_shape], {8: 0, 9: 1, 10: 2, 11: 3}, scratch=[SMEM((SLOTS,), i32)], flops=8_000_000_000,
    )
    density, acceleration, heating, *_ = call(
        last_kernel, "last",
        [(v, SMEM) for v in (own, count, *lists)]
        + [(v, VMEM) for v in (lefts, reaches, supports, yl, yh, ta, tb, tp, sums)],
        [((SLOTS, TILE), f32, VMEM), ((3, SLOTS, TILE), f32, VMEM), ((SLOTS, TILE), f32, VMEM), *tables, sums_shape],
        {11: 3, 12: 4, 13: 5, 14: 6}, flops=1_000_000_000,
    )
    shape_out = (1, 1, 1, SLOTS, TILE)
    return density.reshape(shape_out), acceleration.reshape((3,) + shape_out), heating.reshape(shape_out)


def solution(mesh):
    in_specs = (
        P(None, "gx", "gy", "gz", None),
        P(None, "gx", "gy", "gz", None),
        P("gx", "gy", "gz", None),
        P("gx", "gy", "gz", None),
        P("gx", "gy", "gz", None),
        P("gx", "gy", "gz", None),
        P(),
        P(),
    )
    out_specs = (
        P("gx", "gy", "gz", None, None),
        P(None, "gx", "gy", "gz", None, None),
        P("gx", "gy", "gz", None, None),
    )
    return jax.shard_map(
        on_device, mesh=mesh, in_specs=in_specs, out_specs=out_specs, check_vma=False
    )
```

```python
import functools
import math

import jax
import jax.numpy as jnp
from jax import lax
from jax.experimental import pallas as pl
from jax.experimental.pallas import tpu as pltpu
from jax.sharding import PartitionSpec as P

BRICK = 8
WIDE = BRICK + 4
NEAR = BRICK + 2
ROW = 16
SLOTS = 16
TILE = 128
A_ROWS = WIDE * WIDE * WIDE * 4
B_ROWS = NEAR * NEAR * WIDE * 4
P_ROWS = NEAR * NEAR * ROW
X_ROWS = 2 * 64 * 4 + 64 * 4 + 64
Z_ROWS = 96 * 8 + 80 * 4 + 80
Y_ROWS = 12 * 96 + 10 * 48 + 10 * 16
PAIRS = 512
GROUP = 8
LIMIT = 16 * 1024 * 1024

adiabatic_less_one = 2.0 / 3.0
kernel_norm = 21.0 / (2.0 * math.pi)
density_scale = kernel_norm / (256.0 * TILE)
slope_scale = 20.0 * kernel_norm / (64.0 * TILE)
TINY = 1e-30

bf16 = jnp.bfloat16
f32 = jnp.float32


def a_row(x, y, z):
    return ((x * WIDE + y) * WIDE + z) * 4


def b_row(x, y, z):
    return ((x * NEAR + y) * WIDE + z) * 4


def p_row(x, y, z):
    return (x * NEAR + y) * ROW + ((z + 7) & 15)


def near_id(x, y, z):
    return (x * NEAR + y) * NEAR + z


def rows(ref, start, size, multiple=4):
    return ref[pl.ds(pl.multiple_of(start, multiple), size), :]


def put(ref, start, value, multiple=4):
    ref[pl.ds(pl.multiple_of(start, multiple), value.shape[0]), :] = value


def move(to, to_row, source, row, size):
    to[to_row : to_row + size, :] = source[row : row + size, :]


def pack_x(
    where, cells, counts, fields, own, count, near_counts, near_cells, ta, tb, tp, up, down, held, count_tiles, own_tile, sems
):
    copies = [pltpu.make_async_copy(field, place, sems.at[k]) for k, (field, place) in enumerate(zip(fields, held))]
    for copy in copies:
        copy.start()
    lists = []
    for k in range(9):
        a, b = (where[0] + k // 3 - 1) & 7, (where[1] + k % 3 - 1) & 7
        lists.append(pltpu.make_async_copy(cells.at[a, b], near_cells.at[k], sems.at[6 + k]))
        if k % 3 == 0:
            lists.append(pltpu.make_async_copy(counts.at[a], count_tiles.at[k // 3], sems.at[15 + k // 3]))
    own_copy = pltpu.make_async_copy(cells.at[where[0], where[1]], own_tile, sems.at[18])
    lists.append(own_copy)
    for copy in lists:
        copy.start()
    for copy in lists:
        copy.wait()
    for s in range(SLOTS):
        own[s] = own_tile[where[2], s]
    for k in range(27):
        b, d = (where[1] + k // 3 % 3 - 1) & 7, (where[2] + k % 3 - 1) & 7
        near_counts[k] = count_tiles[k // 9, b, d]
    count[0] = near_counts[13]
    for copy in copies:
        copy.wait()
    off, vel, mass, sup, energy, old = held
    for x in range(BRICK):
        for y in range(BRICK):
            a, b = a_row(x + 2, y + 2, 2), b_row(x + 1, y + 1, 2)
            for f in range(3):
                ta[pl.ds(a + f, BRICK, stride=4), :] = off[f, x, y] - 0.5
                tb[pl.ds(b + f, BRICK, stride=4), :] = vel[f, x, y]
            ta[pl.ds(a + 3, BRICK, stride=4), :] = mass[x, y]
            tb[pl.ds(b + 3, BRICK, stride=4), :] = sup[x, y]
            p = p_row(x + 1, y + 1, 1)
            tp[p : p + BRICK, :] = adiabatic_less_one * energy[x, y] / old[x, y]

    def slot(s, carry):
        x, y, z = slot_place(own, s)
        tp[pl.ds(p_row(x + 1, y + 1, z + 1), 1), :] = -energy[x, y, pl.ds(z, 1), :]
        return carry

    lax.fori_loop(0, count[0], slot, 0)
    for ref, xa, xb in ((up, 8, 8), (down, 2, 1)):
        for y in range(BRICK):
            for layer in range(2):
                move(ref, (layer * 8 + y) * 32, ta, a_row(xa + layer, y + 2, 2), 32)
            move(ref, 512 + y * 32, tb, b_row(xb, y + 1, 2), 32)
            move(ref, 768 + y * 8, tp, p_row(xb, y + 1, 1), 8)


def fill_x(low, high, ta, tb, tp):
    for ref, xa, xb in ((low, 0, 0), (high, 10, 9)):
        for y in range(BRICK):
            for layer in range(2):
                move(ta, a_row(xa + layer, y + 2, 2), ref, (layer * 8 + y) * 32, 32)
            move(tb, b_row(xb, y + 1, 2), ref, 512 + y * 32, 32)
            move(tp, p_row(xb, y + 1, 1), ref, 768 + y * 8, 8)


def pack_z(ta, tb, tp, up, down):
    for ref, za, zb, zp in ((up, 8, 9, 8), (down, 2, 2, 1)):
        for i in range(96):
            move(ref, i * 8, ta, a_row(i // 8, i % 8 + 2, za), 8)
        for i in range(80):
            move(ref, 768 + i * 4, tb, b_row(i // 8, i % 8 + 1, zb), 4)
            move(ref, 1088 + i, tp, p_row(i // 8, i % 8 + 1, zp), 1)


def fill_z(low, high, ta, tb, tp):
    for ref, za, zb, zp in ((low, 0, 1, 0), (high, 10, 10, 9)):
        for i in range(96):
            move(ta, a_row(i // 8, i % 8 + 2, za), ref, i * 8, 8)
        for i in range(80):
            move(tb, b_row(i // 8, i % 8 + 1, zb), ref, 768 + i * 4, 4)
            move(tp, p_row(i // 8, i % 8 + 1, zp), ref, 1088 + i, 1)


def pack_y(ta, tb, tp, up, down):
    for ref, ya, yb in ((up, 8, 8), (down, 2, 1)):
        for x in range(WIDE):
            move(ref, x * 96, ta, a_row(x, ya, 0), 96)
        for x in range(NEAR):
            move(ref, 1152 + x * 48, tb, b_row(x, yb, 0), 48)
            move(ref, 1632 + x * 16, tp, (x * NEAR + yb) * ROW, 16)


def fill_y(low, high, ta, tb, tp):
    for ref, ya, yb in ((low, 0, 0), (high, 10, 9)):
        for x in range(WIDE):
            move(ta, a_row(x, ya, 0), ref, x * 96, 96)
        for x in range(NEAR):
            move(tb, b_row(x, yb, 0), ref, 1152 + x * 48, 48)
            move(tp, (x * NEAR + yb) * ROW, ref, 1632 + x * 16, 16)


def thirds(value):
    high = value.astype(bf16).astype(f32)
    rest = value - high
    middle = rest.astype(bf16).astype(f32)
    return high, middle, rest - middle


def own_side(position, support):
    x, y, z = position[0:1], position[1:2], position[2:3]
    square = x * x + y * y + z * z
    zero = jnp.zeros((3, TILE), f32)
    eight = jnp.concatenate(
        [-32.0 * x, -32.0 * y, -32.0 * z, jnp.full((1, TILE), 16.0, f32), 16.0 * square, zero], axis=0
    )
    first, second, third = thirds(eight)
    four = jnp.concatenate([4.0 * support, jnp.zeros((7, TILE), f32)], axis=0)
    filler = jnp.zeros((TILE - 56, TILE), f32)
    stacked = jnp.concatenate([first, first, first, second, second, third, four, filler], axis=0)
    turned = stacked.T
    reach = jnp.broadcast_to(turned[:, 48:49], (TILE, TILE))
    return turned[:, 0:48].astype(bf16), reach


def distances(square):
    square = jnp.maximum(square, TINY)
    return square * lax.rsqrt(square)


def halves(value):
    high = value.astype(bf16)
    return high, (value - high.astype(f32)).astype(bf16)


def contract(columns, weights):
    return lax.dot_general(columns, weights, (((1,), (1,)), ((), ())), preferred_element_type=f32)


def wide(parts):
    return jnp.concatenate(parts, axis=1)


def tall(parts):
    return jnp.concatenate(parts, axis=0)


def eighth_power(value):
    value = value * value
    value = value * value
    return value * value


def slot_place(own, s):
    cell = own[s]
    return cell >> 6, (cell >> 3) & 7, cell & 7


def lane_sums(value):
    return jnp.sum(value.T, axis=0, keepdims=True)


def place_rows(dx, dy, dz, rank):
    fx, fy, fz = (jnp.asarray(d).astype(f32) for d in (dx, dy, dz))
    return jnp.where(rank == 0, fx, jnp.where(rank == 1, fy, jnp.where(rank == 2, fz, 0.0)))


def other_side(position, eight, rank):
    square = jnp.sum(jnp.where(rank < 3, position * position, 0.0), axis=0, keepdims=True)
    line = lax.broadcasted_iota(jnp.int32, (8, TILE), 0)
    mixed = jnp.where(line < 3, eight, jnp.where(line == 3, square, jnp.where(line == 4, 1.0, 0.0)))
    first, second, third = thirds(mixed)
    return tall([first, second, third, first, second, first]).astype(bf16)


def weigh(weight, base):
    return tall(thirds(weight * base)).astype(bf16)


NEIGHBOURS = [(dx, dy, dz) for dx in (-1, 0, 1) for dy in (-1, 0, 1) for dz in (-1, 0, 1)]
PIECE = 32


def prepare_slots(own, ta, tb, lefts, reaches, supports):
    def group(g, carry):
        for k in range(4):
            s = g * 4 + k
            x, y, z = slot_place(own, s)
            position = rows(ta, a_row(x + 2, y + 2, z + 2), 4)
            support = rows(tb, b_row(x + 1, y + 1, z + 2), 4)[3:4]
            left, reach = own_side(position[0:3], support)
            lefts[s] = left
            reaches[s] = reach
            supports[s] = 0.25 * reach
        return carry

    lax.fori_loop(0, SLOTS // 4, group, 0)


def slot_sums(own, ta, tb, tp, lefts, reaches, supports, sums, s, planes, more):
    x, y, z = slot_place(own, s)
    rank = lax.broadcasted_iota(jnp.int32, (4, TILE), 0)
    line = lax.broadcasted_iota(jnp.int32, (8, TILE), 0)
    centre = rows(tb, b_row(x + 1, y + 1, z + 2), 4)
    drift = jnp.where(rank < 3, jnp.mean(centre, axis=1, keepdims=True), 0.0)
    left = lefts[s]
    total = jnp.zeros((TILE, TILE), f32)
    a_columns, b_columns, a_weights, b_weights, sides = [], [], [], [], []
    for dx, dy, dz in [(dx, dy, dz) for dy in planes for dx in (-1, 0, 1) for dz in (-1, 0, 1)]:
        position = rows(ta, a_row(x + 2 + dx, y + 2 + dy, z + 2 + dz), 4) + place_rows(dx, dy, dz, rank)
        motion = rows(tb, b_row(x + 1 + dx, y + 1 + dy, z + 2 + dz), 4) - drift
        mass, support = position[3:4], motion[3:4]
        pressure = tp[pl.ds(p_row(x + 1 + dx, y + 1 + dy, z + 1 + dz), 1), :]
        still = jnp.maximum(pressure, 0.0)
        inner = jnp.sum(jnp.where(rank < 3, position * motion, 0.0), axis=0, keepdims=True)
        eight = tall([position, motion])
        base = jnp.where(line == 3, 1.0, jnp.where(line == 7, inner, eight))
        a_columns += [weigh(mass, base)] * 2
        b_columns += [weigh(mass * still / eighth_power(support), base)] * 2
        sides.append((other_side(position, eight, rank), mass, 4.0 * support))
    for k, (side, mass, support) in enumerate(sides):
        if k % 2 == 0:
            pair = wide([side, sides[k + 1][0]]) if k + 1 < len(sides) else side
            both = jnp.dot(left, pair, preferred_element_type=f32)
        squares = both[:, (k % 2) * TILE : (k % 2 + 1) * TILE]
        terms, a_high, a_low, b_high, b_low = [], [], [], [], []
        for r in range(0, TILE, PIECE):
            reach = reaches[s, r : r + PIECE, :]
            distance = distances(squares[r : r + PIECE])
            inside = jnp.maximum(reach - distance, 0.0)
            square = inside * inside
            terms.append(square * square * (distance + supports[s, r : r + PIECE, :]) * mass)
            high, low = halves(square * inside)
            a_high.append(high)
            a_low.append(low)
            outer = jnp.maximum(support - distance, 0.0)
            high, low = halves(outer * outer * outer)
            b_high.append(high)
            b_low.append(low)
        total = total + tall(terms)
        a_weights += [tall(a_high), tall(a_low)]
        b_weights += [tall(b_high), tall(b_low)]
    a_sum = contract(wide(a_columns), wide(a_weights))
    b_sum = contract(wide(b_columns), wide(b_weights))
    at = s * 16
    a_sum = a_sum[0:8] + a_sum[8:16] + a_sum[16:24]
    b_sum = jnp.where(line == 7, lane_sums(total), b_sum[0:8] + b_sum[8:16] + b_sum[16:24])
    if more:
        a_sum = a_sum + rows(sums, at, 8, 8)
        b_sum = b_sum + rows(sums, at + 8, 8, 8)
    put(sums, at, a_sum, 8)
    put(sums, at + 8, b_sum, 8)


def active_pairs(pairs, own, ta, tb, tp, lefts, sums, first, size):
    rank = lax.broadcasted_iota(jnp.int32, (4, TILE), 0)
    line = lax.broadcasted_iota(jnp.int32, (8, TILE), 0)
    found = []
    for k in range(size):
        pair = pairs[first + k]
        s, n = pair >> 5, pair & 31
        x, y, z = slot_place(own, s & 15)
        dx, dy, dz = n // 9 - 1, n // 3 % 3 - 1, n % 3 - 1
        position = rows(ta, a_row(x + 2 + dx, y + 2 + dy, z + 2 + dz), 4) + place_rows(dx, dy, dz, rank)
        support = rows(tb, b_row(x + 1 + dx, y + 1 + dy, z + 2 + dz), 4)[3:4]
        pressure = jnp.abs(tp[pl.ds(p_row(x + 1 + dx, y + 1 + dy, z + 1 + dz), 1), :])
        eight = tall([position, jnp.zeros((4, TILE), f32)])
        base = jnp.where(line == 3, 1.0, jnp.where(line < 3, eight, 0.0))
        columns = weigh(position[3:4] * pressure / eighth_power(support), base)
        squares = jnp.dot(lefts[s & 15], other_side(position, eight, rank), preferred_element_type=f32)
        outer = jnp.maximum(4.0 * support - distances(squares), 0.0)
        high, low = halves(outer * outer * outer)
        out = contract(wide([columns, columns]), wide([high, low]))
        found.append((s, out[0:8] + out[8:16] + out[16:24]))
    for s, more in found:
        sums[pl.ds(pl.multiple_of(s * 16 + 8, 8), 4), :] += more[0:4]


def halo_density(ta, tb, tp, x, y, z):
    rank = lax.broadcasted_iota(jnp.int32, (4, TILE), 0)
    centre = rows(ta, a_row(x + 1, y + 1, z + 1), 4)
    support = rows(tb, b_row(x, y, z + 1), 4)[3:4]
    left, reach = own_side(centre[0:3], support)
    total = jnp.zeros((TILE, TILE), f32)
    sides = []
    for dx, dy, dz in NEIGHBOURS:
        position = rows(ta, a_row(x + 1 + dx, y + 1 + dy, z + 1 + dz), 4) + place_rows(dx, dy, dz, rank)
        eight = tall([position, jnp.zeros((4, TILE), f32)])
        sides.append((other_side(position, eight, rank), position[3:4]))
    for k, (side, mass) in enumerate(sides):
        if k % 2 == 0:
            pair = wide([side, sides[k + 1][0]]) if k + 1 < 27 else side
            both = jnp.dot(left, pair, preferred_element_type=f32)
        squares = both[:, (k % 2) * TILE : (k % 2 + 1) * TILE]
        terms = []
        for r in range(0, TILE, PIECE):
            near = reach[r : r + PIECE]
            distance = distances(squares[r : r + PIECE])
            inside = jnp.maximum(near - distance, 0.0)
            square = inside * inside
            terms.append(square * square * (distance + 0.25 * near) * mass)
        total = total + tall(terms)
    density = density_scale * lane_sums(total) / eighth_power(support)
    at = p_row(x, y, z)
    return at, adiabatic_less_one * tp[pl.ds(at, 1), :] / density


def mark_near(where, own, own_count, near_cells, near_counts, marks):
    brick_z = lax.broadcasted_iota(jnp.int32, (BRICK, SLOTS), 0)
    place = lax.broadcasted_iota(jnp.int32, (BRICK, SLOTS), 1)
    dz = ((brick_z - where[2] + 9) & 7) - 1
    listed = []
    for k in range(9):
        cell = near_cells[k]
        counts = [jnp.where(dz == d, near_counts[k * 3 + d + 1], 0) for d in (-1, 0, 1)]
        used = place < counts[0] + counts[1] + counts[2]
        x = (cell >> 6) + (k // 3 - 1) * BRICK
        y = ((cell >> 3) & 7) + (k % 3 - 1) * BRICK
        listed.append((jnp.where(used, x, -99), y, (cell & 7) + dz * BRICK, cell))

    def slot(s, bits):
        ox, oy, oz = slot_place(own, s)
        out = []
        for (x, y, z, _), bit in zip(listed, bits):
            far = jnp.maximum(jnp.maximum(jnp.abs(x - ox), jnp.abs(y - oy)), jnp.abs(z - oz))
            out.append(bit | jnp.where(far == 1, jnp.left_shift(1, s), 0))
        return tuple(out)

    bits = lax.fori_loop(0, own_count, slot, (jnp.zeros((BRICK, SLOTS), jnp.int32),) * 9)
    for k in range(9):
        mark = jnp.where(bits[k] == 0, 0, bits[k] | (listed[k][3] << 16))
        places = jnp.where(bits[k] == 0, 0, jnp.left_shift(1, place)).astype(f32)
        whole = jnp.sum(places, axis=1, keepdims=True).astype(jnp.int32)
        for d in (-1, 0, 1):
            b = k * 3 + d + 1
            marks[b : b + 1, 0:SLOTS] = jnp.sum(jnp.where(dz == d, mark, 0), axis=0, keepdims=True)
            summary = jnp.sum(jnp.where(dz == d, jnp.broadcast_to(whole, (BRICK, SLOTS)), 0), axis=0, keepdims=True)
            marks[b : b + 1, SLOTS : 2 * SLOTS] = summary


def list_near(own, own_count, marks, early, late, pairs, sizes, hits):
    def itself(s, carry):
        pairs[s] = s * 32 + 13
        return carry

    lax.fori_loop(0, own_count, itself, 0)

    def brick(b, at):
        places = marks[b, SLOTS]
        for i in range(SLOTS):
            hits[at] = b * SLOTS + i
            at = at + ((places >> i) & 1)
        return at

    hit_count = lax.fori_loop(0, 27, brick, jnp.int32(0))

    def listed(h, carry):
        at, early_at, late_at = carry
        b, i = hits[h] >> 4, hits[h] & 15
        mark = marks[b, i]
        cell = mark >> 16
        x = (cell >> 6) + (b // 9 - 1) * BRICK
        y = ((cell >> 3) & 7) + (b // 3 % 3 - 1) * BRICK
        z = (cell & 7) + (b % 3 - 1) * BRICK
        outside = jnp.where(b == 13, 0, 1)
        inner = jnp.where((y >= 1) & (y <= 6), 1, 0)
        early[early_at] = near_id(x + 1, y + 1, z + 1)
        late[late_at] = near_id(x + 1, y + 1, z + 1)
        for s in range(SLOTS):
            ox, oy, oz = slot_place(own, s)
            pairs[at] = s * 32 + (x - ox + 1) * 9 + (y - oy + 1) * 3 + z - oz + 1
            at = at + ((mark >> s) & 1)
        return at, early_at + outside * inner, late_at + outside * (1 - inner)

    zero = jnp.int32(0)
    at, early_at, late_at = lax.fori_loop(0, hit_count, listed, (jnp.int32(own_count), zero, zero))
    sizes[0], sizes[1], sizes[2] = early_at, late_at, at
    for k in range(GROUP):
        pairs[at + k] = SLOTS * 32 + 13


def stage_needed(own, s):
    x, y, z = slot_place(own, s)
    edge = lambda v: (v == 0) | (v == BRICK - 1)
    return jnp.where(edge(y), 3, jnp.where(edge(z), 2, jnp.where(edge(x), 1, 0)))


def run_stage(stage, quota, own, count, done, body):
    def slot(s, taken):
        go = (stage_needed(own, s) <= stage) & (done[s] == 0) & (taken < quota)

        @pl.when(go)
        def _():
            body(s, (-1, 0, 1), False)
            done[s] = 1

        return taken + go.astype(jnp.int32)

    lax.fori_loop(0, count[0], slot, jnp.int32(0))


def run_edges(own, count, body, planes, more):
    def slot(s, carry):
        @pl.when(stage_needed(own, s) == 3)
        def _():
            inward = jnp.where(slot_place(own, s)[1] == 0, 1, -1)
            body(s, planes(inward), more)

        return carry

    lax.fori_loop(0, count[0], slot, 0)


def run_halo(ta, tb, tp, found, size):
    def halo(k, carry):
        results = []
        for cell in (found[2 * k], found[jnp.minimum(2 * k + 1, size - 1)]):
            results.append(halo_density(ta, tb, tp, cell // 100, cell // 10 % 10, cell % 10))
        for at, value in results:
            tp[pl.ds(at, 1), :] = value
        return carry

    lax.fori_loop(0, (size + 1) // 2, halo, 0)


def finish_slot(own, count, ta, tb, tp, sums, s, density_out, acceleration_out, heating_out):
    used = s < count[0]
    keep = lambda value: jnp.where(used, value, 0.0)
    x, y, z = slot_place(own, s)
    centre_a = rows(ta, a_row(x + 2, y + 2, z + 2), 4)
    centre_b = rows(tb, b_row(x + 1, y + 1, z + 2), 4)
    a_sum = rows(sums, s * 16, 8, 8)
    b_sum = rows(sums, s * 16 + 8, 8, 8)
    pressure = jnp.abs(tp[pl.ds(p_row(x + 1, y + 1, z + 1), 1), :])
    own_scale = slope_scale * pressure / eighth_power(centre_b[3:4])
    moving = centre_b - jnp.mean(centre_b, axis=1, keepdims=True)
    heat = a_sum[7:8]
    inner = jnp.zeros((1, TILE), f32)
    for f in range(3):
        position, speed = centre_a[f : f + 1], moving[f : f + 1]
        inner = inner + position * speed
        heat = heat - speed * a_sum[f : f + 1] - position * a_sum[4 + f : 5 + f]
        push = own_scale * (position * a_sum[3:4] - a_sum[f : f + 1])
        push = push + slope_scale * (position * b_sum[3:4] - b_sum[f : f + 1])
        acceleration_out[f, pl.ds(s, 1), :] = keep(push)
    heating_out[pl.ds(s, 1), :] = keep(-own_scale * (heat + inner * a_sum[3:4]))
    density_out[pl.ds(s, 1), :] = keep(b_sum[7:8])


SMEM = pltpu.SMEM
VMEM = pltpu.VMEM
i32 = jnp.int32


def call(body, name, inputs, outputs, aliases=(), scratch=(), flops=0, limit=LIMIT):
    return pl.pallas_call(
        body,
        name=name,
        out_shape=[jax.ShapeDtypeStruct(shape, dtype) for shape, dtype, _ in outputs],
        in_specs=[pl.BlockSpec(memory_space=space) for _, space in inputs],
        out_specs=[pl.BlockSpec(memory_space=space) for _, _, space in outputs],
        scratch_shapes=list(scratch),
        input_output_aliases=dict(aliases),
        compiler_params=pltpu.CompilerParams(vmem_limit_bytes=limit),
        cost_estimate=pl.CostEstimate(flops=flops, bytes_accessed=1 << 20, transcendentals=0),
    )(*[array for array, _ in inputs])


def pack_x_kernel(where, cells, counts, *refs):
    pack_x(where, cells, counts, refs[:6], *refs[6:15], refs[15:21], *refs[21:])


def stage0_kernel(
    own, count, near_counts, where, near_cells, ta_in, tb_in, tp_in,
    ta, tb, tp, marks, done, lefts, reaches, supports, sums,
):
    mark_near(where, own, count[0], near_cells, near_counts, marks)
    for s in range(SLOTS):
        done[s] = 0
    prepare_slots(own, ta, tb, lefts, reaches, supports)
    body = functools.partial(slot_sums, own, ta, tb, tp, lefts, reaches, supports, sums)
    run_stage(0, QUOTAS[0], own, count, done, body)


def stage1_kernel(
    own, count, marks, done_in, lefts, reaches, supports, ta_in, tb_in, tp_in, sums_in,
    ta, tb, tp, done, sums, early, late, pairs, sizes, hits,
):
    list_near(own, count[0], marks, early, late, pairs, sizes, hits)
    for s in range(SLOTS):
        done[s] = done_in[s]
    body = functools.partial(slot_sums, own, ta, tb, tp, lefts, reaches, supports, sums)
    run_stage(1, QUOTAS[1], own, count, done, body)


def stage2_kernel(
    own, count, done_in, early, sizes, lefts, reaches, supports, ta_in, tb_in, tp_in, sums_in,
    ta, tb, tp, sums, done,
):
    for s in range(SLOTS):
        done[s] = done_in[s]
    body = functools.partial(slot_sums, own, ta, tb, tp, lefts, reaches, supports, sums)
    run_stage(2, SLOTS, own, count, done, body)
    run_edges(own, count, body, lambda inward: (0, inward), False)
    run_halo(ta, tb, tp, early, sizes[0])


def pack_kernel(fill, pack, low, high, ta_in, tb_in, tp_in, ta, tb, tp, up, down):
    fill(low, high, ta, tb, tp)
    pack(ta, tb, tp, up, down)


def last_kernel(
    own, count, late, sizes, pairs, lefts, reaches, supports, yl, yh,
    ta_in, tb_in, tp_in, sums_in, density_out, acceleration_out, heating_out, ta, tb, tp, sums,
):
    fill_y(yl, yh, ta, tb, tp)
    body = functools.partial(slot_sums, own, ta, tb, tp, lefts, reaches, supports, sums)
    run_edges(own, count, body, lambda inward: (-inward,), True)
    run_halo(ta, tb, tp, late, sizes[1])

    def renew(g, carry):
        for s in (g * 4, g * 4 + 1, g * 4 + 2, g * 4 + 3):
            x, y, z = slot_place(own, s)
            at = p_row(x + 1, y + 1, z + 1)
            support = rows(tb, b_row(x + 1, y + 1, z + 2), 4)[3:4]
            density = density_scale * sums[pl.ds(s * 16 + 15, 1), :] / eighth_power(support)
            sums[pl.ds(s * 16 + 15, 1), :] = density
            tp[pl.ds(at, 1), :] = adiabatic_less_one * tp[pl.ds(at, 1), :] / density
        return carry

    lax.fori_loop(0, SLOTS // 4, renew, 0)

    def some_pairs(g, carry):
        active_pairs(pairs, own, ta, tb, tp, lefts, sums, g * GROUP, GROUP)
        return carry

    lax.fori_loop(0, (sizes[2] + GROUP - 1) // GROUP, some_pairs, 0)

    def finish(g, carry):
        for s in (g * 4, g * 4 + 1, g * 4 + 2, g * 4 + 3):
            finish_slot(own, count, ta, tb, tp, sums, s, density_out, acceleration_out, heating_out)
        return carry

    lax.fori_loop(0, SLOTS // 4, finish, 0)


QUOTAS = (3, 4)


def shift_both(axis, up, down):
    devices = lax.axis_size(axis)
    higher = [(i, (i + 1) % devices) for i in range(devices)]
    lower = [(j, i) for i, j in higher]
    return lax.ppermute(up, axis, higher), lax.ppermute(down, axis, lower)


def on_device(offsets, velocity, mass, support, energy, old_density, active_cells, active_count):
    where = jnp.stack([lax.axis_index(a) for a in ("gx", "gy", "gz")]).astype(i32)
    grow = lambda n: ((n, TILE), f32, VMEM)
    tables = [grow(A_ROWS), grow(B_ROWS), grow(P_ROWS)]
    fields = [offsets, velocity, mass, support, energy, old_density]
    stay = lambda array: pltpu.with_memory_space_constraint(array, pltpu.HBM)
    fields = [stay(field) for field in fields]
    scalars = lambda n: ((n,), i32, SMEM)
    near_shape = ((9, BRICK, SLOTS), i32, VMEM)
    own, count, near_counts, near_cells, ta, tb, tp, up, down = call(
        pack_x_kernel, "pack_x",
        [(where, SMEM), (stay(active_cells), pltpu.HBM), (stay(active_count), pltpu.HBM)] + [(f, pltpu.HBM) for f in fields],
        [scalars(SLOTS), scalars(1), scalars(27), near_shape, *tables, grow(X_ROWS), grow(X_ROWS)],
        scratch=[VMEM(f.shape, f32) for f in fields]
        + [SMEM((3, BRICK, BRICK), i32), SMEM((BRICK, SLOTS), i32), pltpu.SemaphoreType.DMA((19,))],
    )
    xl, xh = shift_both("gx", up, down)
    slot_tables = [((SLOTS, TILE, 48), bf16, VMEM), ((SLOTS, TILE, TILE), f32, VMEM), ((SLOTS, TILE, TILE), f32, VMEM)]
    sums_shape = grow((SLOTS + 1) * 16)
    ta, tb, tp, marks, done, lefts, reaches, supports, sums = call(
        stage0_kernel, "stage0",
        [(own, SMEM), (count, SMEM), (near_counts, SMEM), (where, SMEM)]
        + [(near_cells, VMEM), (ta, VMEM), (tb, VMEM), (tp, VMEM)],
        [*tables, ((32, 2 * SLOTS), i32, VMEM), scalars(SLOTS), *slot_tables, sums_shape],
        {5: 0, 6: 1, 7: 2}, flops=8_000_000_000,
    )

    def packed(fill, pack, name, low, high, ta, tb, tp, length):
        return call(
            functools.partial(pack_kernel, fill, pack), name, [(v, VMEM) for v in (low, high, ta, tb, tp)],
            [*tables, grow(length), grow(length)], {2: 0, 3: 1, 4: 2},
        )

    ta, tb, tp, up, down = packed(fill_x, pack_z, "pack_z", xl, xh, ta, tb, tp, Z_ROWS)
    zl, zh = shift_both("gz", up, down)
    ta, tb, tp, done, sums, early, late, pairs, sizes = call(
        stage1_kernel, "stage1",
        [(v, SMEM) for v in (own, count, marks, done)]
        + [(v, VMEM) for v in (lefts, reaches, supports, ta, tb, tp, sums)],
        [*tables, scalars(SLOTS), sums_shape, scalars(512), scalars(512), scalars(PAIRS), scalars(3)],
        {7: 0, 8: 1, 9: 2, 10: 4}, scratch=[SMEM((512,), i32)], flops=8_000_000_000,
    )
    ta, tb, tp, up, down = packed(fill_z, pack_y, "pack_y", zl, zh, ta, tb, tp, Y_ROWS)
    yl, yh = shift_both("gy", up, down)
    ta, tb, tp, sums = call(
        stage2_kernel, "stage2",
        [(v, SMEM) for v in (own, count, done, early, sizes)]
        + [(v, VMEM) for v in (lefts, reaches, supports, ta, tb, tp, sums)],
        [*tables, sums_shape], {8: 0, 9: 1, 10: 2, 11: 3}, scratch=[SMEM((SLOTS,), i32)], flops=8_000_000_000,
    )
    density, acceleration, heating, *_ = call(
        last_kernel, "last",
        [(v, SMEM) for v in (own, count, late, sizes, pairs)]
        + [(v, VMEM) for v in (lefts, reaches, supports, yl, yh, ta, tb, tp, sums)],
        [((SLOTS, TILE), f32, VMEM), ((3, SLOTS, TILE), f32, VMEM), ((SLOTS, TILE), f32, VMEM), *tables, sums_shape],
        {10: 3, 11: 4, 12: 5, 13: 6}, flops=1_000_000_000,
    )
    shape_out = (1, 1, 1, SLOTS, TILE)
    return density.reshape(shape_out), acceleration.reshape((3,) + shape_out), heating.reshape(shape_out)


def solution(mesh):
    in_specs = (
        P(None, "gx", "gy", "gz", None),
        P(None, "gx", "gy", "gz", None),
        P("gx", "gy", "gz", None),
        P("gx", "gy", "gz", None),
        P("gx", "gy", "gz", None),
        P("gx", "gy", "gz", None),
        P(),
        P(),
    )
    out_specs = (
        P("gx", "gy", "gz", None, None),
        P(None, "gx", "gy", "gz", None, None),
        P("gx", "gy", "gz", None, None),
    )
    return jax.shard_map(
        on_device, mesh=mesh, in_specs=in_specs, out_specs=out_specs, check_vma=False
    )
```
